512 devices in a mesh: up: 32 (over y, x), lo: 16 (over z, core).
Axes of the slice: x: 4, y: 8, z: 8, core: 2. Of those that a mesh axis runs over, the one named last changes fastest.
Arguments:
- sector_sizes: int32 [8], replicated, may hold values from 1 to 384, 2048 in all
- left: bfloat16 [9, 384, 3072], P(None, 'lo', 'up'), may hold values from -6 to 6
- upper_edge: bfloat16 [9, 384, 3072], P(None, 'up', 'lo'), may hold values from -0.3125 to 0.3125
- lower_edge: bfloat16 [9, 384, 3072], P(None, 'up', 'lo'), may hold values from -0.109375 to 0.109375
- site_block: float32 [9, 9, 9, 9], replicated, may hold values from -1.5 to 1.5
Outputs:
- right: bfloat16 [9, 384, 3072], P(None, 'lo', 'up')
The draws below stay inside these ranges and needn't reach their ends.
Inputs may be any that keep to these rules, and one draw needn't show every extreme that they name: `sector_sizes`: the 8 sector sizes sum to 2048, and the largest equals 384.
All inputs are finite; a program needn't handle non-finite values.
Results may differ from the reference program's by a relative error of at most 0.022.
Values may be sent and summed in bfloat16 or wider, within the bound.
No kernel may reach another device: no remote copies, remote signals or barrier semaphores. Data moves between devices by JAX's collectives and lax.ppermute only.
A program may use at most 128 MiB of HBM per device.

```python
import math
import jax
import jax.numpy as jnp
import numpy as np
from jax import lax

CHI = 2048
SEC = 8
CAP = 384
DD = 9
N_LO = 16


def steps_of(own_key, shape, shards, least, high):
    def one(dim, blocks):
        draws = jax.random.uniform(jax.random.fold_in(jax.random.fold_in(own_key, 6), dim), (blocks,), jnp.float32, least / len(shards), high / len(shards))
        return jnp.repeat(jnp.exp(draws), shape[dim] // blocks).reshape((-1,) + (1,) * (len(shape) - dim - 1))

    loudness = one(*shards[0])
    for cut in shards[1:]:
        loudness = loudness * one(*cut)
    return loudness


def length_profile(count, total, reach, lean):
    loads = [(1 << 20) // math.isqrt(grade ** lean) + 1 for grade in range(2, count + 1)]
    rest, counts = total - reach - (count - 1), [1] * (count - 1)
    while rest > 0:
        movable = [i for i in range(count - 1) if counts[i] < reach]
        whole, budget = sum([loads[i] for i in movable]), rest
        for i in movable:
            addition = min(reach - counts[i], max(1, budget * loads[i] // whole), rest)
            counts[i] = counts[i] + addition
            rest = rest - addition
    return np.array([reach] + counts)


def uneven_parts(stream_key, number_of, total, limit, skew):
    if number_of == 2:
        one = jax.random.randint(stream_key, (), max(1, total - limit), min(limit, total - 1) + 1)
        return jnp.stack([one, total - one])
    sizes = jnp.asarray(length_profile(number_of, total, limit, skew), jnp.int32)
    pairs = (number_of - 1) // 2
    source_of, receiver = sizes[1:1 + 2 * pairs:2], sizes[2:2 + 2 * pairs:2]
    margin = jnp.minimum(source_of - 1, limit - receiver)
    moved = jax.random.randint(jax.random.fold_in(stream_key, 1), (pairs,), 0, 1 << 20) % (margin + 1)
    sizes = sizes.at[1:1 + 2 * pairs:2].set(source_of - moved).at[2:2 + 2 * pairs:2].set(receiver + moved)
    return sizes[jax.random.permutation(jax.random.fold_in(stream_key, 2), number_of)]


def bell_draw(stream_key, shape, spread, bound, shards=(), kind=jnp.bfloat16):
    entries = spread * jax.random.normal(stream_key, shape, jnp.float32)
    if shards:
        entries = entries * steps_of(stream_key, shape, shards, -0.22, 0.18)
    return jnp.clip(entries, -bound, bound).astype(kind)


def setup_inputs(seed: int = 0) -> dict:
    keys = jax.random.split(jax.random.key(seed), 6)
    return {
        "sector_sizes": uneven_parts(keys[0], SEC, CHI, CAP, 2).astype(jnp.int32),
        "left": bell_draw(keys[1], (DD, CAP, SEC * CAP), 1.0, 6.0, ((1, 16), (2, 32))),
        "upper_edge": bell_draw(keys[2], (DD, CAP, SEC * CAP), CAP ** -0.5, 0.3125, ((1, 32), (2, 16))),
        "lower_edge": bell_draw(keys[3], (DD, CAP, SEC * CAP), (DD * CAP) ** -0.5, 0.109375, ((1, 32), (2, 16))),
        "site_block": bell_draw(keys[4], (DD, DD, DD, DD), 16 ** -0.5, 1.5, (), jnp.float32),
    }


def charge_list():
    return [(member // 3) - (member % 3) for member in range(DD)]


def allowed(sector_sizes, charges, row_ids, col_ids):
    slot_in = col_ids // SEC
    sector_in = col_ids % SEC
    labels = jnp.arange(SEC, dtype=jnp.int32)
    lookup_in = jnp.sum(jnp.where(sector_in[:, None] == labels[None, :], sector_sizes[None, :], 0), axis=1)
    live_in = slot_in < lookup_in
    sector_out = sector_in[None, :] + charges[:, None]
    lookup_out = jnp.sum(jnp.where(sector_out[:, :, None] == labels[None, None, :], sector_sizes[None, None, :], 0), axis=2)
    live_out = row_ids[None, :, None] < lookup_out[:, None, :]
    return live_in[None, None, :] & live_out


def site_allowed(charges):
    charge_up = charges[:, None, None, None]
    charge_left = charges[None, :, None, None]
    charge_right = charges[None, None, :, None]
    charge_down = charges[None, None, None, :]
    return charge_up + charge_right == charge_left + charge_down


def move_sectors(values, amount):
    if amount == 0:
        return values
    filler = jnp.zeros(values.shape[:-1] + (abs(amount),), values.dtype)
    if amount > 0:
        return jnp.concatenate([filler, values[..., :-amount]], axis=-1)
    return jnp.concatenate([values[..., -amount:], filler], axis=-1)


def contract_lower(lower_slab, mixture, shifts):
    pieces = [None] * DD
    for charge_level in sorted(set(shifts)):
        members = [member for member in range(DD) if shifts[member] == charge_level]
        chosen = jnp.stack([move_sectors(lower_slab[member], shifts[member] - charge_level) for member in range(DD)])
        picked = jnp.stack([mixture[member] for member in members])
        summed = jnp.einsum("lyjq,pljxq->pyxq", chosen.astype(jnp.float32), picked.astype(jnp.float32), precision=lax.Precision.HIGHEST)
        for position, member in enumerate(members):
            pieces[member] = summed[position]
    return jnp.stack(pieces)


def reference(sector_sizes, left, upper_edge, lower_edge, site_block):
    shifts = charge_list()
    charges = jnp.array(shifts, dtype=jnp.int32)
    keep_mask = allowed(sector_sizes, charges, jnp.arange(CAP, dtype=jnp.int32), jnp.arange(SEC * CAP, dtype=jnp.int32))
    naught = jnp.zeros((), jnp.bfloat16)
    vector = jnp.where(keep_mask, left, naught)
    upper_tensor = jnp.where(keep_mask, upper_edge, naught).reshape(DD, CAP, CAP, SEC).astype(jnp.float32)
    lower_tensor = jnp.where(keep_mask, lower_edge, naught).reshape(DD, CAP, CAP, SEC)
    site_tensor = jnp.where(site_allowed(charges), site_block, jnp.float32(0.0))
    block_width = CAP // N_LO

    def one_block(running, block_index):
        offset = (block_index * block_width).astype(jnp.int32)
        slab_vec = lax.dynamic_slice_in_dim(vector, offset, block_width, 1).reshape(DD, block_width, CAP, SEC).astype(jnp.float32)
        product = jnp.einsum("kxiq,sjiq->ksjxq", upper_tensor, slab_vec, precision=lax.Precision.HIGHEST)
        product = jnp.stack([move_sectors(product[member], shifts[member]) for member in range(DD)])
        mixture = jnp.einsum("kspl,ksjxq->pljxq", site_tensor, product, precision=lax.Precision.HIGHEST).astype(jnp.bfloat16)
        lower_slab = lax.dynamic_slice_in_dim(lower_tensor, offset, block_width, 2)
        partial_value = contract_lower(lower_slab, mixture, shifts)
        rounded = lax.optimization_barrier(partial_value.astype(jnp.bfloat16))
        return running + rounded.astype(jnp.float32), None

    running, _ = lax.scan(one_block, jnp.zeros((DD, CAP, CAP, SEC), jnp.float32), jnp.arange(N_LO, dtype=jnp.int32))
    return running.reshape(DD, CAP, SEC * CAP).astype(jnp.bfloat16)
```

```python
import jax
import jax.numpy as jnp
from jax import lax
from jax.experimental import pallas as pl
from jax.experimental.pallas import tpu as pltpu
from jax.sharding import PartitionSpec as P

SEC = 8
DD = 9
NX = 4
NY = 8
N_UP = NX * NY
N_LO = 16
XB = 12
JB = 24
CAP = 384
CHARGE = [member // 3 - member % 3 for member in range(DD)]
ORDER = [0, 1, 2, 3, 5, 4, 6, 7, 8]


def places(charge):
    free = [(q, a) for q in range(SEC) for a in range(SEC) if not 0 <= q + charge[ORDER[a]] < SEC]
    found = [None] * SEC
    for q in range(SEC):
        own = [spot for spot in free if spot[0] == q]
        if own:
            found[q] = own[0]
            free.remove(own[0])
    for q in range(SEC):
        if found[q] is None:
            found[q] = free.pop(0)
    return found


IN_PLACES = places(CHARGE)
OUT_PLACES = places([-c for c in CHARGE])
BF = jnp.bfloat16
F32 = jnp.float32
VMEM = pl.BlockSpec(memory_space=pltpu.VMEM)
SMEM = pl.BlockSpec(memory_space=pltpu.SMEM)
PARAMS = pltpu.CompilerParams(vmem_limit_bytes=56 * 1024 * 1024)


def nt(a, b):
    return lax.dot_general(a, b, (((1,), (1,)), ((), ())), preferred_element_type=F32)


def nn(a, b):
    return lax.dot_general(a, b, (((1,), (0,)), ((), ())), preferred_element_type=F32)


def tn(a, b):
    return lax.dot_general(a, b, (((0,), (0,)), ((), ())), preferred_element_type=F32)


def iota(shape, axis):
    return lax.broadcasted_iota(jnp.int32, shape, axis)


def one_hot(flag):
    return jnp.where(flag, 1.0, 0.0).astype(BF)


def sizes_by_sector(sizes_ref, sector, charge):
    found = jnp.zeros(sector.shape, jnp.int32)
    for q in range(SEC):
        if 0 <= q + charge < SEC:
            found = jnp.where(sector == q, sizes_ref[q + charge], found)
    return found


def prepare_kernel(sizes, place, left, upper, lower, lb_out, u_out, left_s, up_s, wide_s, pack):
    up, lo = place[0], place[1]
    lane = iota((1, XB * SEC), 1)
    live = up * XB + lane // SEC < sizes_by_sector(sizes, lane % SEC, 0)
    row = lo * JB + iota((JB, 1), 0)
    limit = {c: sizes_by_sector(sizes, lane % SEC, c) for c in sorted(set(CHARGE))}
    for a, s in enumerate(ORDER):
        keep = live & (row < limit[CHARGE[s]])
        left_s[a * JB:(a + 1) * JB, :] = jnp.where(keep, left[s].astype(F32), 0.0)
    a, b = iota((96, 96), 0), iota((96, 96), 1)
    order = one_hot(b == (a % XB) * SEC + a // XB)
    grid = nt(order, left_s[...].astype(BF))
    pack[0] = grid[:, 0:192]
    for q, (host, at) in enumerate(IN_PLACES):
        pack[0, host * XB:(host + 1) * XB, at * JB:(at + 1) * JB] = grid[q * XB:(q + 1) * XB, 192:216]
    lane = iota((1, JB * SEC), 1)
    live = lo * JB + lane // SEC < sizes_by_sector(sizes, lane % SEC, 0)
    row = up * XB + iota((XB, 1), 0)
    limit = {c: sizes_by_sector(sizes, lane % SEC, c) for c in sorted(set(CHARGE))}
    blank = jnp.zeros((4, JB * SEC), F32)
    for k in range(DD):
        keep = live & (row < limit[CHARGE[k]])
        up_s[0, k * 16:k * 16 + XB, :] = jnp.where(keep, upper[k].astype(F32), 0.0)
        up_s[0, k * 16 + XB:(k + 1) * 16, :] = blank
        up_s[1, k * 16:k * 16 + XB, :] = jnp.where(keep, lower[k].astype(F32), 0.0)
        up_s[1, k * 16 + XB:(k + 1) * 16, :] = blank
    a, b = iota((128, 144), 0), iota((128, 144), 1)
    dense = nn(one_hot((b == (a // XB) * 16 + a % XB) & (a < 108)), up_s[0].astype(BF)).astype(BF)
    a, b = iota((192, 192), 0), iota((192, 192), 1)
    edge = nt(one_hot(b == (a % JB) * SEC + a // JB), dense).astype(BF)
    a, b = iota((96, 144), 0), iota((96, 144), 1)
    lower_16 = up_s[1].astype(BF)
    sector = iota((96, 192), 0) // XB
    column = iota((96, 192), 1) % SEC
    for n, l in enumerate(ORDER):
        copies = nn(one_hot(b == l * 16 + a % XB), lower_16)
        wide_s[:, n * 256:n * 256 + 192] = jnp.where(
            column == sector - CHARGE[l], copies, 0.0
        ).astype(BF)
        wide_s[:, n * 256 + 192:(n + 1) * 256] = jnp.zeros((96, 64), BF)
    a, b = iota((DD * 256, 256), 0), iota((DD * 256, 256), 1)
    fold = one_hot(b == (a // 256) * JB + (a % 256) // SEC)
    grid = nn(wide_s[...], fold)
    pack[1] = grid[:, 0:192]
    for v, (host, at) in enumerate(OUT_PLACES):
        pack[1, host * XB:(host + 1) * XB, at * JB:(at + 1) * JB] = grid[v * XB:(v + 1) * XB, 192:216]
    ours = pack[0].astype(BF)
    theirs = pack[1].astype(BF)
    for n in range(NY):
        lb_out[n, 0:96, :] = ours[:, 0:128]
        lb_out[n, 96:192, :] = theirs[:, 0:128]
        lb_out[n, 192:288, 0:64] = ours[:, 128:192]
        lb_out[n, 192:288, 64:128] = theirs[:, 128:192]
    u_out[...] = edge


def prepare(sizes, place, left, upper, lower):
    return pl.pallas_call(
        prepare_kernel,
        out_shape=(
            jax.ShapeDtypeStruct((NY, 288, 128), BF),
            jax.ShapeDtypeStruct((192, 128), BF),
        ),
        in_specs=[SMEM, SMEM, VMEM, VMEM, VMEM],
        out_specs=(VMEM, VMEM),
        scratch_shapes=[
            pltpu.VMEM((216, 96), F32),
            pltpu.VMEM((2, 144, 192), F32),
            pltpu.VMEM((96, DD * 256), BF),
            pltpu.VMEM((2, 96, 192), F32),
        ],
        compiler_params=PARAMS,
        name="prepare",
    )(sizes, place, left, upper, lower)


def lanes_of(at, side):
    start = at * JB
    return side * 128 + start if start + JB <= 128 else 256 + side * 64 + start - 128


def main_kernel(site, lb, u, out, left_q, lower_v, image, at, mixed, spread):
    a, b = iota((384, 384), 0), iota((384, 384), 1)
    regroup = one_hot(b == ((a % 48) // XB) * 96 + (a // 48) * XB + a % XB)
    lane = iota((1, 256), 1) // JB
    zero = jnp.zeros((), BF)
    left_q[...] = jnp.zeros(left_q.shape, BF)
    lower_v[...] = jnp.zeros(lower_v.shape, BF)
    for g in range(NY):
        block = jnp.concatenate(
            [lb[:, g, 96 * n:96 * (n + 1), :].reshape(384, 128) for n in range(3)], axis=1
        )
        part = nn(regroup, block).astype(BF)
        rows = slice(g * 48, (g + 1) * 48)
        for q in range(SEC):
            near = part[q * 48:(q + 1) * 48, 0:128]
            far = part[q * 48:(q + 1) * 48, 256:320]
            empty = [n for n in range(SEC) if not 0 <= q + CHARGE[ORDER[n]] < SEC]
            for n in empty:
                near = jnp.where(lane[:, 0:128] == n, zero, near)
                far = jnp.where(lane[:, 128:192] == n, zero, far)
            left_q[q, rows, 0:128] = near
            left_q[q, rows, 128:192] = far
            host, spot = IN_PLACES[q]
            start = lanes_of(spot, 0)
            left_q[q, rows, 192:216] = part[host * 48:(host + 1) * 48, start:start + JB]
        for v in range(SEC):
            near = part[v * 48:(v + 1) * 48, 128:256]
            far = part[v * 48:(v + 1) * 48, 320:384]
            empty = [n for n in range(SEC) if not 0 <= v - CHARGE[ORDER[n]] < SEC]
            for n in empty:
                near = jnp.where(lane[:, 0:128] == n, zero, near)
                far = jnp.where(lane[:, 128:192] == n, zero, far)
            lower_v[rows, v * 256:v * 256 + 128] = near
            lower_v[rows, v * 256 + 128:v * 256 + 192] = far
            host, spot = OUT_PLACES[v]
            start = lanes_of(spot, 1)
            lower_v[rows, v * 256 + 192:v * 256 + 216] = part[host * 48:(host + 1) * 48, start:start + JB]
    for q in range(SEC):
        columns = u[:, q * JB:(q + 1) * JB, :].reshape(CAP, 128)
        image[q * 128:(q + 1) * 128, :] = tn(columns, left_q[q]).astype(BF)
    a, b = iota((96, 1024), 0), iota((96, 1024), 1)
    p, x = a // XB, a % XB
    for k in range(DD):
        q = p - CHARGE[k]
        pick = one_hot((b == q * 128 + k * XB + x) & (q >= 0) & (q < SEC))
        at[:, k * 256:(k + 1) * 256] = nn(pick, image[...]).astype(BF)
    a, b = iota((81, DD * 256), 0), iota((81, DD * 256), 1)
    pos = (b % 256) // JB
    s = jnp.where(pos == 4, ORDER[4], jnp.where(pos == 5, ORDER[5], pos))
    widen = one_hot((s + (b // 256) * DD == a) & (pos < DD))
    weights = nn(site[...].astype(BF), widen)
    a, b = iota((JB, DD * 256), 0), iota((JB, DD * 256), 1)
    same = ((b % 256) % JB == a) & (b % 256 < 216)
    mixed[216:256, :] = jnp.zeros((40, SEC * 96), BF)
    last = None
    for n, r in enumerate(ORDER):
        rows = [
            jnp.where(same, weights[r * DD + l:r * DD + l + 1, :], 0.0).astype(BF) for l in ORDER
        ]
        last = nt(jnp.concatenate(rows, axis=0), at[...]).astype(BF)
        if n < SEC:
            mixed[0:216, n * 96:(n + 1) * 96] = last
    for p, (host, spot) in enumerate(IN_PLACES):
        start = spot * 96 + host * XB
        mixed[0:216, start:start + XB] = last[:, p * XB:(p + 1) * XB]
    lane = iota((1, SEC * 96), 1)
    sector = (lane % 96) // XB
    for n in range(SEC):
        sector = jnp.where(lane // 96 == n, sector + CHARGE[ORDER[n]], sector)
    for p, (host, spot) in enumerate(IN_PLACES):
        sector = jnp.where(lane // XB == spot * SEC + host, p, sector)
    for v in range(SEC):
        spread[v * 256:(v + 1) * 256, :] = jnp.where(sector == v, mixed[...], zero)
    for n in range(3):
        cut = slice(n * 256, (n + 1) * 256)
        out[:, cut] = nn(lower_v[...], spread[:, cut]).astype(BF)


def main(site, lb, u):
    return pl.pallas_call(
        main_kernel,
        out_shape=jax.ShapeDtypeStruct((CAP, SEC * 96), BF),
        in_specs=[VMEM] * 3,
        out_specs=VMEM,
        scratch_shapes=[
            pltpu.VMEM((SEC, CAP, 256), BF),
            pltpu.VMEM((CAP, SEC * 256), BF),
            pltpu.VMEM((SEC * 128, 256), BF),
            pltpu.VMEM((96, DD * 256), BF),
            pltpu.VMEM((256, SEC * 96), BF),
            pltpu.VMEM((SEC * 256, SEC * 96), BF),
        ],
        compiler_params=PARAMS,
        name="main",
    )(site, lb, u)


def finish_kernel(terms, out, stacked):
    total = terms[0].astype(F32)
    for z in range(1, N_LO):
        total = total + terms[z].astype(F32)
    for n in range(SEC):
        r = ORDER[n]
        stacked[r * JB:(r + 1) * JB, :] = total[:, n * 96:(n + 1) * 96]
    for p, (host, spot) in enumerate(IN_PLACES):
        start = spot * 96 + host * XB
        stacked[SEC * JB:DD * JB, p * XB:(p + 1) * XB] = total[:, start:start + XB]
    a, b = iota((96, 96), 0), iota((96, 96), 1)
    turned = nn(stacked[...].astype(BF), one_hot(b == (a % XB) * SEC + a // XB))
    p = iota((1, 96), 1) % SEC
    for r in range(DD):
        keep = (p + CHARGE[r] >= 0) & (p + CHARGE[r] < SEC)
        out[r] = jnp.where(keep, turned[r * JB:(r + 1) * JB, :], 0.0).astype(BF)


def finish(terms):
    return pl.pallas_call(
        finish_kernel,
        out_shape=jax.ShapeDtypeStruct((DD, JB, 96), BF),
        in_specs=[VMEM],
        out_specs=VMEM,
        scratch_shapes=[pltpu.VMEM((DD * JB, 96), F32)],
        compiler_params=PARAMS,
        name="finish",
    )(terms)


X_GROUPS = [[y * NX + x for x in range(NX)] for y in range(NY)]
Y_GROUPS = [[y * NX + x for y in range(NY)] for x in range(NX)]


def local(sector_sizes, left, upper_edge, lower_edge, site_block):
    charges = jnp.array(CHARGE, dtype=jnp.int32)
    place = jnp.stack([lax.axis_index("up"), lax.axis_index("lo")]).astype(jnp.int32)
    even = (
        charges[:, None, None, None] + charges[None, None, :, None]
        == charges[None, :, None, None] + charges[None, None, None, :]
    )
    site = jnp.where(even, site_block, jnp.float32(0.0))
    site = site.transpose(2, 3, 0, 1).reshape(81, 81)
    lb, u = prepare(sector_sizes, place, left, upper_edge, lower_edge)
    line = lax.all_to_all(lb, "up", 0, 0, axis_index_groups=Y_GROUPS)
    line, u, site = lax.optimization_barrier((line, u, site))
    whole = lax.all_to_all(
        jnp.broadcast_to(line, (NX,) + line.shape), "up", 0, 0, axis_index_groups=X_GROUPS
    )
    u = lax.all_gather(u, "lo", axis=0)
    terms = main(site, whole, u)
    terms = lax.all_to_all(terms.reshape(N_LO, JB, SEC * 96), "lo", 0, 0)
    return finish(terms)


def solution(mesh):
    return jax.shard_map(
        local,
        mesh=mesh,
        in_specs=(P(), P(None, "lo", "up"), P(None, "up", "lo"), P(None, "up", "lo"), P()),
        out_specs=P(None, "lo", "up"),
        check_vma=False,
    )
```

```python
import jax
import jax.numpy as jnp
from jax import lax
from jax.experimental import pallas as pl
from jax.experimental.pallas import tpu as pltpu
from jax.sharding import PartitionSpec as P

SEC = 8
DD = 9
NX = 4
NY = 8
N_UP = NX * NY
N_LO = 16
XB = 12
JB = 24
CAP = 384
CHARGE = [member // 3 - member % 3 for member in range(DD)]
ORDER = [0, 1, 2, 3, 5, 4, 6, 7, 8]


def places(charge):
    free = [(q, a) for q in range(SEC) for a in range(SEC) if not 0 <= q + charge[ORDER[a]] < SEC]
    found = [None] * SEC
    for q in range(SEC):
        own = [spot for spot in free if spot[0] == q]
        if own:
            found[q] = own[0]
            free.remove(own[0])
    for q in range(SEC):
        if found[q] is None:
            found[q] = free.pop(0)
    return found


IN_PLACES = places(CHARGE)
OUT_PLACES = places([-c for c in CHARGE])
BF = jnp.bfloat16
F32 = jnp.float32
VMEM = pl.BlockSpec(memory_space=pltpu.VMEM)
SMEM = pl.BlockSpec(memory_space=pltpu.SMEM)
PARAMS = pltpu.CompilerParams(vmem_limit_bytes=16 * 1024 * 1024)
WIDE = pltpu.CompilerParams(vmem_limit_bytes=56 * 1024 * 1024)


def nt(a, b):
    return lax.dot_general(a, b, (((1,), (1,)), ((), ())), preferred_element_type=F32)


def nn(a, b):
    return lax.dot_general(a, b, (((1,), (0,)), ((), ())), preferred_element_type=F32)


def tn(a, b):
    return lax.dot_general(a, b, (((0,), (0,)), ((), ())), preferred_element_type=F32)


def iota(shape, axis):
    return lax.broadcasted_iota(jnp.int32, shape, axis)


def one_hot(flag):
    return jnp.where(flag, 1.0, 0.0).astype(BF)


def sizes_by_sector(sizes_ref, sector, charge):
    found = jnp.zeros(sector.shape, jnp.int32)
    for q in range(SEC):
        if 0 <= q + charge < SEC:
            found = jnp.where(sector == q, sizes_ref[q + charge], found)
    return found


def prepare_kernel(sizes, left, upper, lower, lb_out, u_out, left_s, up_s, wide_s, pack):
    up, lo = lax.axis_index("up"), lax.axis_index("lo")
    lane = iota((1, XB * SEC), 1)
    live = up * XB + lane // SEC < sizes_by_sector(sizes, lane % SEC, 0)
    row = lo * JB + iota((JB, 1), 0)
    limit = {c: sizes_by_sector(sizes, lane % SEC, c) for c in sorted(set(CHARGE))}
    for a, s in enumerate(ORDER):
        keep = live & (row < limit[CHARGE[s]])
        left_s[a * JB:(a + 1) * JB, :] = jnp.where(keep, left[s].astype(F32), 0.0)
    a, b = iota((96, 96), 0), iota((96, 96), 1)
    order = one_hot(b == (a % XB) * SEC + a // XB)
    grid = nt(order, left_s[...].astype(BF))
    pack[0] = grid[:, 0:192]
    for q, (host, at) in enumerate(IN_PLACES):
        pack[0, host * XB:(host + 1) * XB, at * JB:(at + 1) * JB] = grid[q * XB:(q + 1) * XB, 192:216]
    lane = iota((1, JB * SEC), 1)
    live = lo * JB + lane // SEC < sizes_by_sector(sizes, lane % SEC, 0)
    row = up * XB + iota((XB, 1), 0)
    limit = {c: sizes_by_sector(sizes, lane % SEC, c) for c in sorted(set(CHARGE))}
    blank = jnp.zeros((4, JB * SEC), F32)
    for k in range(DD):
        keep = live & (row < limit[CHARGE[k]])
        up_s[0, k * 16:k * 16 + XB, :] = jnp.where(keep, upper[k].astype(F32), 0.0)
        up_s[0, k * 16 + XB:(k + 1) * 16, :] = blank
        up_s[1, k * 16:k * 16 + XB, :] = jnp.where(keep, lower[k].astype(F32), 0.0)
        up_s[1, k * 16 + XB:(k + 1) * 16, :] = blank
    a, b = iota((128, 144), 0), iota((128, 144), 1)
    dense = nn(one_hot((b == (a // XB) * 16 + a % XB) & (a < 108)), up_s[0].astype(BF)).astype(BF)
    a, b = iota((192, 192), 0), iota((192, 192), 1)
    edge = nt(one_hot(b == (a % JB) * SEC + a // JB), dense).astype(BF)
    a, b = iota((96, 144), 0), iota((96, 144), 1)
    lower_16 = up_s[1].astype(BF)
    sector = iota((96, 192), 0) // XB
    column = iota((96, 192), 1) % SEC
    for n, l in enumerate(ORDER):
        copies = nn(one_hot(b == l * 16 + a % XB), lower_16)
        wide_s[:, n * 256:n * 256 + 192] = jnp.where(
            column == sector - CHARGE[l], copies, 0.0
        ).astype(BF)
        wide_s[:, n * 256 + 192:(n + 1) * 256] = jnp.zeros((96, 64), BF)
    a, b = iota((DD * 256, 256), 0), iota((DD * 256, 256), 1)
    fold = one_hot(b == (a // 256) * JB + (a % 256) // SEC)
    grid = nn(wide_s[...], fold)
    pack[1] = grid[:, 0:192]
    for v, (host, at) in enumerate(OUT_PLACES):
        pack[1, host * XB:(host + 1) * XB, at * JB:(at + 1) * JB] = grid[v * XB:(v + 1) * XB, 192:216]
    ours = pack[0].astype(BF)
    theirs = pack[1].astype(BF)
    for n in range(NY):
        lb_out[n, 0:96, :] = ours[:, 0:128]
        lb_out[n, 96:192, :] = theirs[:, 0:128]
        lb_out[n, 192:288, 0:64] = ours[:, 128:192]
        lb_out[n, 192:288, 64:128] = theirs[:, 128:192]
    u_out[...] = edge


def prepare(sizes, left, upper, lower):
    return pl.pallas_call(
        prepare_kernel,
        out_shape=(
            jax.ShapeDtypeStruct((NY, 288, 128), BF),
            jax.ShapeDtypeStruct((192, 128), BF),
        ),
        in_specs=[SMEM, VMEM, VMEM, VMEM],
        out_specs=(VMEM, VMEM),
        scratch_shapes=[
            pltpu.VMEM((216, 96), F32),
            pltpu.VMEM((2, 144, 192), F32),
            pltpu.VMEM((96, DD * 256), BF),
            pltpu.VMEM((2, 96, 192), F32),
        ],
        compiler_params=WIDE,
        name="prepare",
    )(sizes, left, upper, lower)


def regrouping(turn):
    a, b = iota((384, 384), 0), iota((384, 384), 1)
    x = ((a % 48) // XB + turn) % NX
    return one_hot(b == x * 96 + (a // 48) * XB + a % XB)


def spread_out(part, charge, hosts, sector):
    lane = iota((1, 192), 1) // JB
    rows = part[sector * 48:(sector + 1) * 48]
    for n in range(SEC):
        if not 0 <= sector + charge[ORDER[n]] < SEC:
            rows = jnp.where(lane == n, jnp.zeros((), BF), rows)
    host, spot = hosts[sector]
    return rows, part[host * 48:(host + 1) * 48, spot * JB:(spot + 1) * JB]


def main_kernel(site, lb, u, ours, theirs, left_q, lower_v, moved, at, mixed, spread, wide):
    regroup_left = regrouping(0)
    regroup_lower = regrouping(2 * lax.rem(lax.axis_index("lo"), 2))
    left_q[...] = jnp.zeros(left_q.shape, BF)
    lower_v[...] = jnp.zeros(lower_v.shape, BF)
    moved[...] = jnp.zeros(moved.shape, F32)
    for g in range(NY):
        near, other, far = [lb[:, g, 96 * n:96 * (n + 1), :].reshape(384, 128) for n in range(3)]
        rows = slice(g * 48, (g + 1) * 48)
        part = nn(regroup_left, jnp.concatenate([near, far[:, 0:64]], axis=1)).astype(BF)
        for q in range(SEC):
            own, last = spread_out(part, CHARGE, IN_PLACES, q)
            left_q[q, rows, 0:192] = own
            left_q[q, rows, 192:216] = last
        part = nn(regroup_lower, jnp.concatenate([other, far[:, 64:128]], axis=1)).astype(BF)
        for v in range(SEC):
            own, last = spread_out(part, [-c for c in CHARGE], OUT_PLACES, v)
            lower_v[rows, v * 256:v * 256 + 192] = own
            lower_v[rows, v * 256 + 192:v * 256 + 216] = last
    for q in range(SEC):
        columns = u[:, q * JB:(q + 1) * JB, :].reshape(CAP, 128)
        image = tn(columns, left_q[q])
        for k in range(DD):
            p = q + CHARGE[k]
            if 0 <= p < SEC:
                moved[p * XB:(p + 1) * XB, k * 256:(k + 1) * 256] = image[k * XB:(k + 1) * XB]
    at[...] = moved[...].astype(BF)
    a, b = iota((81, DD * 256), 0), iota((81, DD * 256), 1)
    pos = (b % 256) // JB
    s = jnp.where(pos == 4, ORDER[4], jnp.where(pos == 5, ORDER[5], pos))
    widen = one_hot((s + (b // 256) * DD == a) & (pos < DD))
    wide[...] = nn(site[...].astype(BF), widen)
    a, b = iota((JB, DD * 256), 0), iota((JB, DD * 256), 1)
    same = ((b % 256) % JB == a) & (b % 256 < 216)
    mixed[216:256, :] = jnp.zeros((40, SEC * 96), BF)
    last = None
    for n, r in enumerate(ORDER):
        rows = [jnp.where(same, wide[r * DD + l:r * DD + l + 1, :], 0.0).astype(BF) for l in ORDER]
        last = nt(jnp.concatenate(rows, axis=0), at[...]).astype(BF)
        if n < SEC:
            mixed[0:216, n * 96:(n + 1) * 96] = last
    for p, (host, spot) in enumerate(IN_PLACES):
        start = spot * 96 + host * XB
        mixed[0:216, start:start + XB] = last[:, p * XB:(p + 1) * XB]
    lane = iota((1, SEC * 96), 1)
    sector = (lane % 96) // XB
    for n in range(SEC):
        sector = jnp.where(lane // 96 == n, sector + CHARGE[ORDER[n]], sector)
    for p, (host, spot) in enumerate(IN_PLACES):
        sector = jnp.where(lane // XB == spot * SEC + host, p, sector)
    for v in range(SEC):
        spread[v * 256:(v + 1) * 256, :] = jnp.where(sector == v, mixed[...], jnp.zeros((), BF))
    for n in range(3):
        cut = slice(n * 256, (n + 1) * 256)
        total = nn(lower_v[...], spread[:, cut])
        for g in range(NY):
            ours[g, :, cut] = total[g * 48:g * 48 + 24]
            theirs[g, :, cut] = total[g * 48 + 24:(g + 1) * 48].astype(BF)


def main(site, lb, u):
    return pl.pallas_call(
        main_kernel,
        out_shape=(
            jax.ShapeDtypeStruct((NY, JB, SEC * 96), F32),
            jax.ShapeDtypeStruct((NY, JB, SEC * 96), BF),
        ),
        in_specs=[VMEM] * 3,
        out_specs=(VMEM, VMEM),
        scratch_shapes=[
            pltpu.VMEM((SEC, CAP, 256), BF),
            pltpu.VMEM((CAP, SEC * 256), BF),
            pltpu.VMEM((96, DD * 256), F32),
            pltpu.VMEM((96, DD * 256), BF),
            pltpu.VMEM((256, SEC * 96), BF),
            pltpu.VMEM((SEC * 256, SEC * 96), BF),
            pltpu.VMEM((81, DD * 256), F32),
        ],
        compiler_params=PARAMS,
        name="main",
    )(site, lb, u)


def finish_kernel(terms, out, stacked):
    total = terms[0].astype(F32)
    for z in range(1, N_LO // 2):
        total = total + terms[z].astype(F32)
    for n in range(SEC):
        r = ORDER[n]
        stacked[r * JB:(r + 1) * JB, :] = total[:, n * 96:(n + 1) * 96]
    for p, (host, spot) in enumerate(IN_PLACES):
        start = spot * 96 + host * XB
        stacked[SEC * JB:DD * JB, p * XB:(p + 1) * XB] = total[:, start:start + XB]
    a, b = iota((96, 96), 0), iota((96, 96), 1)
    turned = nn(stacked[...].astype(BF), one_hot(b == (a % XB) * SEC + a // XB))
    p = iota((1, 96), 1) % SEC
    for r in range(DD):
        keep = (p + CHARGE[r] >= 0) & (p + CHARGE[r] < SEC)
        out[r] = jnp.where(keep, turned[r * JB:(r + 1) * JB, :], 0.0).astype(BF)


def finish(terms):
    return pl.pallas_call(
        finish_kernel,
        out_shape=jax.ShapeDtypeStruct((DD, JB, 96), BF),
        in_specs=[VMEM],
        out_specs=VMEM,
        scratch_shapes=[pltpu.VMEM((DD * JB, 96), F32)],
        compiler_params=PARAMS,
        name="finish",
    )(terms)


Z_GROUPS = [[2 * z + core for z in range(N_LO // 2)] for core in range(2)]
X_GROUPS = [[y * NX + x for x in range(NX)] for y in range(NY)]
Y_GROUPS = [[y * NX + x for y in range(NY)] for x in range(NX)]


def local(sector_sizes, left, upper_edge, lower_edge, site_block):
    charges = jnp.array(CHARGE, dtype=jnp.int32)
    lb, u = prepare(sector_sizes, left, upper_edge, lower_edge)
    site_block, lb = lax.optimization_barrier((site_block, lb))
    even = (
        charges[:, None, None, None] + charges[None, None, :, None]
        == charges[None, :, None, None] + charges[None, None, None, :]
    )
    site = jnp.where(even, site_block, jnp.float32(0.0))
    site = site.transpose(2, 3, 0, 1).reshape(81, 81)
    line = lax.all_to_all(lb, "up", 0, 0, axis_index_groups=Y_GROUPS)
    line, u, site = lax.optimization_barrier((line, u, site))
    whole = lax.all_to_all(
        jnp.broadcast_to(line, (NX,) + line.shape), "up", 0, 0, axis_index_groups=X_GROUPS
    )
    u = lax.all_gather(u, "lo", axis=0)
    ours, theirs = main(site, whole, u)
    swap = [(n, n + 1 - 2 * (n % 2)) for n in range(N_LO)]
    theirs = lax.ppermute(theirs, "lo", swap)
    terms = (ours + theirs.astype(F32)).astype(BF)
    terms = lax.all_to_all(terms, "lo", 0, 0, axis_index_groups=Z_GROUPS)
    return finish(terms)


def solution(mesh):
    return jax.shard_map(
        local,
        mesh=mesh,
        in_specs=(P(), P(None, "lo", "up"), P(None, "up", "lo"), P(None, "up", "lo"), P()),
        out_specs=P(None, "lo", "up"),
        check_vma=False,
    )
```

```python
import jax
import jax.numpy as jnp
from jax import lax
from jax.experimental import pallas as pl
from jax.experimental.pallas import tpu as pltpu
from jax.sharding import PartitionSpec as P

SEC = 8
DD = 9
NX = 4
NY = 8
N_UP = NX * NY
N_LO = 16
XB = 12
JB = 24
CAP = 384
CHARGE = [member // 3 - member % 3 for member in range(DD)]
ORDER = [0, 1, 2, 3, 5, 4, 6, 7, 8]


def places(charge):
    free = [(q, a) for q in range(SEC) for a in range(SEC) if not 0 <= q + charge[ORDER[a]] < SEC]
    found = [None] * SEC
    for q in range(SEC):
        own = [spot for spot in free if spot[0] == q]
        if own:
            found[q] = own[0]
            free.remove(own[0])
    for q in range(SEC):
        if found[q] is None:
            found[q] = free.pop(0)
    return found


IN_PLACES = places(CHARGE)
OUT_PLACES = places([-c for c in CHARGE])
BF = jnp.bfloat16
F32 = jnp.float32
VMEM = pl.BlockSpec(memory_space=pltpu.VMEM)
SMEM = pl.BlockSpec(memory_space=pltpu.SMEM)
PARAMS = pltpu.CompilerParams(vmem_limit_bytes=16 * 1024 * 1024)
WIDE = pltpu.CompilerParams(vmem_limit_bytes=56 * 1024 * 1024)


def nt(a, b):
    return lax.dot_general(a, b, (((1,), (1,)), ((), ())), preferred_element_type=F32)


def nn(a, b):
    return lax.dot_general(a, b, (((1,), (0,)), ((), ())), preferred_element_type=F32)


def tn(a, b):
    return lax.dot_general(a, b, (((0,), (0,)), ((), ())), preferred_element_type=F32)


def iota(shape, axis):
    return lax.broadcasted_iota(jnp.int32, shape, axis)


def one_hot(flag):
    return jnp.where(flag, 1.0, 0.0).astype(BF)


def sizes_by_sector(sizes_ref, sector, charge):
    found = jnp.zeros(sector.shape, jnp.int32)
    for q in range(SEC):
        if 0 <= q + charge < SEC:
            found = jnp.where(sector == q, sizes_ref[q + charge], found)
    return found


def prepare_kernel(sizes, left, upper, lower, lb_out, u_out, left_s, up_s, wide_s, pack):
    up, lo = lax.axis_index("up"), lax.axis_index("lo")
    lane = iota((1, XB * SEC), 1)
    live = up * XB + lane // SEC < sizes_by_sector(sizes, lane % SEC, 0)
    row = lo * JB + iota((JB, 1), 0)
    limit = {c: sizes_by_sector(sizes, lane % SEC, c) for c in sorted(set(CHARGE))}
    for a, s in enumerate(ORDER):
        keep = live & (row < limit[CHARGE[s]])
        left_s[a * JB:(a + 1) * JB, :] = jnp.where(keep, left[s].astype(F32), 0.0)
    a, b = iota((96, 96), 0), iota((96, 96), 1)
    order = one_hot(b == (a % XB) * SEC + a // XB)
    grid = nt(order, left_s[...].astype(BF))
    pack[0] = grid[:, 0:192]
    for q, (host, at) in enumerate(IN_PLACES):
        pack[0, host * XB:(host + 1) * XB, at * JB:(at + 1) * JB] = grid[q * XB:(q + 1) * XB, 192:216]
    lane = iota((1, JB * SEC), 1)
    live = lo * JB + lane // SEC < sizes_by_sector(sizes, lane % SEC, 0)
    row = up * XB + iota((XB, 1), 0)
    limit = {c: sizes_by_sector(sizes, lane % SEC, c) for c in sorted(set(CHARGE))}
    blank = jnp.zeros((4, JB * SEC), F32)
    for k in range(DD):
        keep = live & (row < limit[CHARGE[k]])
        up_s[0, k * 16:k * 16 + XB, :] = jnp.where(keep, upper[k].astype(F32), 0.0)
        up_s[0, k * 16 + XB:(k + 1) * 16, :] = blank
        up_s[1, k * 16:k * 16 + XB, :] = jnp.where(keep, lower[k].astype(F32), 0.0)
        up_s[1, k * 16 + XB:(k + 1) * 16, :] = blank
    a, b = iota((128, 144), 0), iota((128, 144), 1)
    dense = nn(one_hot((b == (a // XB) * 16 + a % XB) & (a < 108)), up_s[0].astype(BF)).astype(BF)
    a, b = iota((192, 192), 0), iota((192, 192), 1)
    edge = nt(one_hot(b == (a % JB) * SEC + a // JB), dense).astype(BF)
    a, b = iota((96, 144), 0), iota((96, 144), 1)
    lower_16 = up_s[1].astype(BF)
    sector = iota((96, 192), 0) // XB
    column = iota((96, 192), 1) % SEC
    for n, l in enumerate(ORDER):
        copies = nn(one_hot(b == l * 16 + a % XB), lower_16)
        wide_s[:, n * 256:n * 256 + 192] = jnp.where(
            column == sector - CHARGE[l], copies, 0.0
        ).astype(BF)
        wide_s[:, n * 256 + 192:(n + 1) * 256] = jnp.zeros((96, 64), BF)
    a, b = iota((DD * 256, 256), 0), iota((DD * 256, 256), 1)
    fold = one_hot(b == (a // 256) * JB + (a % 256) // SEC)
    grid = nn(wide_s[...], fold)
    pack[1] = grid[:, 0:192]
    for v, (host, at) in enumerate(OUT_PLACES):
        pack[1, host * XB:(host + 1) * XB, at * JB:(at + 1) * JB] = grid[v * XB:(v + 1) * XB, 192:216]
    for n in range(NY):
        for side in range(2):
            lb_out[n, side, 0:96, :] = pack[side, :, 0:128].astype(BF)
            lb_out[n, side, 96:144, 0:64] = pack[side, 0:48, 128:192].astype(BF)
            lb_out[n, side, 96:144, 64:128] = pack[side, 48:96, 128:192].astype(BF)
    u_out[...] = edge


def prepare(sizes, left, upper, lower):
    return pl.pallas_call(
        prepare_kernel,
        out_shape=(
            jax.ShapeDtypeStruct((NY, 2, 144, 128), BF),
            jax.ShapeDtypeStruct((192, 128), BF),
        ),
        in_specs=[SMEM, VMEM, VMEM, VMEM],
        out_specs=(VMEM, VMEM),
        scratch_shapes=[
            pltpu.VMEM((216, 96), F32),
            pltpu.VMEM((2, 144, 192), F32),
            pltpu.VMEM((96, DD * 256), BF),
            pltpu.VMEM((2, 96, 192), F32),
        ],
        compiler_params=WIDE,
        name="prepare",
    )(sizes, left, upper, lower)


def regrouping(turn):
    a, b = iota((384, 384), 0), iota((384, 384), 1)
    d = ((a % 48) // XB + turn + NX - lax.axis_index("up") % NX) % NX
    return one_hot(b == d * 96 + (a // 48) * XB + a % XB)


def regrouped(regroup, pieces, g):
    lines = [piece[g] for piece in pieces]
    near = jnp.concatenate([line[0:96, :] for line in lines], axis=0)
    far = jnp.concatenate(
        [line[96:144, 64 * h:64 * (h + 1)] for line in lines for h in range(2)], axis=0
    )
    return nn(regroup, jnp.concatenate([near, far], axis=1)).astype(BF)


def spread_out(part, charge, hosts, sector):
    lane = iota((1, 192), 1) // JB
    rows = part[sector * 48:(sector + 1) * 48]
    for n in range(SEC):
        if not 0 <= sector + charge[ORDER[n]] < SEC:
            rows = jnp.where(lane == n, jnp.zeros((), BF), rows)
    host, spot = hosts[sector]
    return rows, part[host * 48:(host + 1) * 48, spot * JB:(spot + 1) * JB]


def mix_kernel(site, u, own, right, far, left, mixed, left_q, moved, at, wide):
    regroup = regrouping(0)
    left_q[...] = jnp.zeros(left_q.shape, BF)
    moved[...] = jnp.zeros(moved.shape, F32)
    for g in range(NY):
        part = regrouped(regroup, (own, right, far, left), g)
        for q in range(SEC):
            rows, last = spread_out(part, CHARGE, IN_PLACES, q)
            left_q[q, g * 48:(g + 1) * 48, 0:192] = rows
            left_q[q, g * 48:(g + 1) * 48, 192:216] = last
    for q in range(SEC):
        columns = u[:, q * JB:(q + 1) * JB, :].reshape(CAP, 128)
        image = tn(columns, left_q[q])
        for k in range(DD):
            p = q + CHARGE[k]
            if 0 <= p < SEC:
                moved[p * XB:(p + 1) * XB, k * 256:(k + 1) * 256] = image[k * XB:(k + 1) * XB]
    at[...] = moved[...].astype(BF)
    a, b = iota((81, DD * 256), 0), iota((81, DD * 256), 1)
    pos = (b % 256) // JB
    s = jnp.where(pos == 4, ORDER[4], jnp.where(pos == 5, ORDER[5], pos))
    widen = one_hot((s + (b // 256) * DD == a) & (pos < DD))
    wide[...] = nn(site[...].astype(BF), widen)
    a, b = iota((JB, DD * 256), 0), iota((JB, DD * 256), 1)
    same = ((b % 256) % JB == a) & (b % 256 < 216)
    mixed[216:256, :] = jnp.zeros((40, SEC * 96), BF)
    last = None
    for n, r in enumerate(ORDER):
        rows = [jnp.where(same, wide[r * DD + l:r * DD + l + 1, :], 0.0).astype(BF) for l in ORDER]
        last = nt(jnp.concatenate(rows, axis=0), at[...]).astype(BF)
        if n < SEC:
            mixed[0:216, n * 96:(n + 1) * 96] = last
    for p, (host, spot) in enumerate(IN_PLACES):
        start = spot * 96 + host * XB
        mixed[0:216, start:start + XB] = last[:, p * XB:(p + 1) * XB]


def mix(site, u, pieces):
    return pl.pallas_call(
        mix_kernel,
        out_shape=jax.ShapeDtypeStruct((256, SEC * 96), BF),
        in_specs=[VMEM] * 6,
        out_specs=VMEM,
        scratch_shapes=[
            pltpu.VMEM((SEC, CAP, 256), BF),
            pltpu.VMEM((96, DD * 256), F32),
            pltpu.VMEM((96, DD * 256), BF),
            pltpu.VMEM((81, DD * 256), F32),
        ],
        compiler_params=PARAMS,
        cost_estimate=pl.CostEstimate(flops=6_000_000_000, bytes_accessed=3_000_000, transcendentals=0),
        name="mix",
    )(site, u, *pieces)


def lower_kernel(mixed, own, right, far, left, ours, theirs, lower_v, spread):
    regroup = regrouping(2 * lax.rem(lax.axis_index("lo"), 2))
    lower_v[...] = jnp.zeros(lower_v.shape, BF)
    for g in range(NY):
        part = regrouped(regroup, (own, right, far, left), g)
        for v in range(SEC):
            rows, last = spread_out(part, [-c for c in CHARGE], OUT_PLACES, v)
            lower_v[g * 48:(g + 1) * 48, v * 256:v * 256 + 192] = rows
            lower_v[g * 48:(g + 1) * 48, v * 256 + 192:v * 256 + 216] = last
    lane = iota((1, SEC * 96), 1)
    sector = (lane % 96) // XB
    for n in range(SEC):
        sector = jnp.where(lane // 96 == n, sector + CHARGE[ORDER[n]], sector)
    for p, (host, spot) in enumerate(IN_PLACES):
        sector = jnp.where(lane // XB == spot * SEC + host, p, sector)
    for v in range(SEC):
        spread[v * 256:(v + 1) * 256, :] = jnp.where(sector == v, mixed[...], jnp.zeros((), BF))
    for n in range(3):
        cut = slice(n * 256, (n + 1) * 256)
        total = nn(lower_v[...], spread[:, cut])
        for g in range(NY):
            ours[g, :, cut] = total[g * 48:g * 48 + 24]
            theirs[g, :, cut] = total[g * 48 + 24:(g + 1) * 48].astype(BF)


def contract_lower(mixed, pieces):
    return pl.pallas_call(
        lower_kernel,
        out_shape=(
            jax.ShapeDtypeStruct((NY, JB, SEC * 96), F32),
            jax.ShapeDtypeStruct((NY, JB, SEC * 96), BF),
        ),
        in_specs=[VMEM] * 5,
        out_specs=(VMEM, VMEM),
        scratch_shapes=[
            pltpu.VMEM((CAP, SEC * 256), BF),
            pltpu.VMEM((SEC * 256, SEC * 96), BF),
        ],
        compiler_params=PARAMS,
        name="lower",
    )(mixed, *pieces)


def finish_kernel(terms, out, stacked):
    total = terms[0].astype(F32)
    for z in range(1, N_LO // 2):
        total = total + terms[z].astype(F32)
    for n in range(SEC):
        r = ORDER[n]
        stacked[r * JB:(r + 1) * JB, :] = total[:, n * 96:(n + 1) * 96]
    for p, (host, spot) in enumerate(IN_PLACES):
        start = spot * 96 + host * XB
        stacked[SEC * JB:DD * JB, p * XB:(p + 1) * XB] = total[:, start:start + XB]
    a, b = iota((96, 96), 0), iota((96, 96), 1)
    turned = nn(stacked[...].astype(BF), one_hot(b == (a % XB) * SEC + a // XB))
    p = iota((1, 96), 1) % SEC
    for r in range(DD):
        keep = (p + CHARGE[r] >= 0) & (p + CHARGE[r] < SEC)
        out[r] = jnp.where(keep, turned[r * JB:(r + 1) * JB, :], 0.0).astype(BF)


def finish(terms):
    return pl.pallas_call(
        finish_kernel,
        out_shape=jax.ShapeDtypeStruct((DD, JB, 96), BF),
        in_specs=[VMEM],
        out_specs=VMEM,
        scratch_shapes=[pltpu.VMEM((DD * JB, 96), F32)],
        compiler_params=PARAMS,
        name="finish",
    )(terms)


Z_GROUPS = [[2 * z + core for z in range(N_LO // 2)] for core in range(2)]
Y_GROUPS = [[y * NX + x for y in range(NY)] for x in range(NX)]


def from_x(value, d):
    pairs = [(y * NX + x, y * NX + (x - d) % NX) for y in range(NY) for x in range(NX)]
    return lax.ppermute(value, "up", pairs)


def local(sector_sizes, left, upper_edge, lower_edge, site_block):
    charges = jnp.array(CHARGE, dtype=jnp.int32)
    lb, u = prepare(sector_sizes, left, upper_edge, lower_edge)
    site_block, lb = lax.optimization_barrier((site_block, lb))
    even = (
        charges[:, None, None, None] + charges[None, None, :, None]
        == charges[None, :, None, None] + charges[None, None, None, :]
    )
    site = jnp.where(even, site_block, jnp.float32(0.0))
    site = site.transpose(2, 3, 0, 1).reshape(81, 81)
    line = lax.all_to_all(lb, "up", 0, 0, axis_index_groups=Y_GROUPS)
    u = lax.all_gather(u, "lo", axis=0)
    line, u, site = lax.optimization_barrier((line, u, site))
    left, lower = line[:, 0], line[:, 1]
    left_right, left_left = from_x(left, 1), from_x(left, -1)
    lower_right, lower_left = from_x(lower, 1), from_x(lower, -1)
    left_far, lower_far = from_x(left_right, 1), from_x(lower_left, -1)
    mixed = mix(site, u, (left, left_right, left_far, left_left))
    ours, theirs = contract_lower(mixed, (lower, lower_right, lower_far, lower_left))
    swap = [(n, n + 1 - 2 * (n % 2)) for n in range(N_LO)]
    theirs = lax.ppermute(theirs, "lo", swap)
    terms = (ours + theirs.astype(F32)).astype(BF)
    terms = lax.all_to_all(terms, "lo", 0, 0, axis_index_groups=Z_GROUPS)
    return finish(terms)


def solution(mesh):
    return jax.shard_map(
        local,
        mesh=mesh,
        in_specs=(P(), P(None, "lo", "up"), P(None, "up", "lo"), P(None, "up", "lo"), P()),
        out_specs=P(None, "lo", "up"),
        check_vma=False,
    )
```

```python
import functools

import jax
import jax.numpy as jnp
from jax import lax
from jax.experimental import pallas as pl
from jax.experimental.pallas import tpu as pltpu
from jax.sharding import PartitionSpec as P

SEC = 8
DD = 9
NX = 4
NY = 8
N_UP = NX * NY
N_LO = 16
XB = 12
JB = 24
CAP = 384
CHARGE = [member // 3 - member % 3 for member in range(DD)]
ORDER = [0, 1, 2, 3, 5, 4, 6, 7, 8]


def places(charge):
    free = [(q, a) for q in range(SEC) for a in range(SEC) if not 0 <= q + charge[ORDER[a]] < SEC]
    found = [None] * SEC
    for q in range(SEC):
        own = [spot for spot in free if spot[0] == q]
        if own:
            found[q] = own[0]
            free.remove(own[0])
    for q in range(SEC):
        if found[q] is None:
            found[q] = free.pop(0)
    return found


IN_PLACES = places(CHARGE)
OUT_PLACES = places([-c for c in CHARGE])
BF = jnp.bfloat16
F32 = jnp.float32
VMEM = pl.BlockSpec(memory_space=pltpu.VMEM)
SMEM = pl.BlockSpec(memory_space=pltpu.SMEM)
PARAMS = pltpu.CompilerParams(vmem_limit_bytes=16 * 1024 * 1024)
WIDE = pltpu.CompilerParams(vmem_limit_bytes=56 * 1024 * 1024)


def nt(a, b):
    return lax.dot_general(a, b, (((1,), (1,)), ((), ())), preferred_element_type=F32)


def nn(a, b):
    return lax.dot_general(a, b, (((1,), (0,)), ((), ())), preferred_element_type=F32)


def tn(a, b):
    return lax.dot_general(a, b, (((0,), (0,)), ((), ())), preferred_element_type=F32)


def iota(shape, axis):
    return lax.broadcasted_iota(jnp.int32, shape, axis)


def one_hot(flag):
    return jnp.where(flag, 1.0, 0.0).astype(BF)


def sizes_by_sector(sizes_ref, sector, charge):
    found = jnp.zeros(sector.shape, jnp.int32)
    for q in range(SEC):
        if 0 <= q + charge < SEC:
            found = jnp.where(sector == q, sizes_ref[q + charge], found)
    return found


def prepare_kernel(sizes, left, upper, lower, lb_out, u_out, left_s, up_s, wide_s, pack):
    up, lo = lax.axis_index("up"), lax.axis_index("lo")
    lane = iota((1, XB * SEC), 1)
    live = up * XB + lane // SEC < sizes_by_sector(sizes, lane % SEC, 0)
    row = lo * JB + iota((JB, 1), 0)
    limit = {c: sizes_by_sector(sizes, lane % SEC, c) for c in sorted(set(CHARGE))}
    for a, s in enumerate(ORDER):
        keep = live & (row < limit[CHARGE[s]])
        left_s[a * JB:(a + 1) * JB, :] = jnp.where(keep, left[s].astype(F32), 0.0)
    a, b = iota((96, 96), 0), iota((96, 96), 1)
    order = one_hot(b == (a % XB) * SEC + a // XB)
    grid = nt(order, left_s[...].astype(BF))
    pack[0] = grid[:, 0:192]
    for q, (host, at) in enumerate(IN_PLACES):
        pack[0, host * XB:(host + 1) * XB, at * JB:(at + 1) * JB] = grid[q * XB:(q + 1) * XB, 192:216]
    lane = iota((1, JB * SEC), 1)
    live = lo * JB + lane // SEC < sizes_by_sector(sizes, lane % SEC, 0)
    row = up * XB + iota((XB, 1), 0)
    limit = {c: sizes_by_sector(sizes, lane % SEC, c) for c in sorted(set(CHARGE))}
    blank = jnp.zeros((4, JB * SEC), F32)
    for k in range(DD):
        keep = live & (row < limit[CHARGE[k]])
        up_s[0, k * 16:k * 16 + XB, :] = jnp.where(keep, upper[k].astype(F32), 0.0)
        up_s[0, k * 16 + XB:(k + 1) * 16, :] = blank
        up_s[1, k * 16:k * 16 + XB, :] = jnp.where(keep, lower[k].astype(F32), 0.0)
        up_s[1, k * 16 + XB:(k + 1) * 16, :] = blank
    a, b = iota((128, 144), 0), iota((128, 144), 1)
    dense = nn(one_hot((b == (a // XB) * 16 + a % XB) & (a < 108)), up_s[0].astype(BF)).astype(BF)
    a, b = iota((192, 192), 0), iota((192, 192), 1)
    edge = nt(one_hot(b == (a % JB) * SEC + a // JB), dense).astype(BF)
    a, b = iota((DD * 96, 144), 0), iota((DD * 96, 144), 1)
    pos = a // 96
    l = jnp.where(pos == 4, ORDER[4], jnp.where(pos == 5, ORDER[5], pos))
    copies = nn(one_hot(b == l * 16 + a % XB), up_s[1].astype(BF))
    sector = iota((96, 192), 0) // XB - iota((96, 192), 1) % SEC
    for n, l in enumerate(ORDER):
        wide_s[n * 96:(n + 1) * 96, :] = jnp.where(
            sector == CHARGE[l], copies[n * 96:(n + 1) * 96], 0.0
        ).astype(BF)
    a, b = iota((192, 128), 0), iota((192, 128), 1)
    folded = nn(wide_s[...], one_hot(b == a // SEC))
    for n in range(SEC):
        pack[1, :, n * JB:(n + 1) * JB] = folded[n * 96:(n + 1) * 96, 0:JB]
    for v, (host, at) in enumerate(OUT_PLACES):
        row = SEC * 96 + v * XB
        pack[1, host * XB:(host + 1) * XB, at * JB:(at + 1) * JB] = folded[row:row + XB, 0:JB]
    for n in range(NY):
        for side in range(2):
            lb_out[n, side, 0:96, :] = pack[side, :, 0:128].astype(BF)
            lb_out[n, side, 96:144, 0:64] = pack[side, 0:48, 128:192].astype(BF)
            lb_out[n, side, 96:144, 64:128] = pack[side, 48:96, 128:192].astype(BF)
    u_out[...] = edge


def prepare(sizes, left, upper, lower):
    return pl.pallas_call(
        prepare_kernel,
        out_shape=(
            jax.ShapeDtypeStruct((NY, 2, 144, 128), BF),
            jax.ShapeDtypeStruct((192, 128), BF),
        ),
        in_specs=[SMEM, VMEM, VMEM, VMEM],
        out_specs=(VMEM, VMEM),
        scratch_shapes=[
            pltpu.VMEM((216, 96), F32),
            pltpu.VMEM((2, 144, 192), F32),
            pltpu.VMEM((DD * 96, 192), BF),
            pltpu.VMEM((2, 96, 192), F32),
        ],
        compiler_params=WIDE,
        name="prepare",
    )(sizes, left, upper, lower)


def charge_of(member):
    return member // 3 - member % 3


def regrouping(turn, count):
    a, b = iota((count * 96, 384), 0), iota((count * 96, 384), 1)
    size = count * XB
    d = ((a % size) // XB + turn + NX - lax.axis_index("up") % NX) % NX
    return one_hot(b == d * 96 + (a // size) * XB + a % XB)


def regrouped(regroup, pieces, g):
    lines = [piece[g] for piece in pieces]
    near = jnp.concatenate([line[0:96, :] for line in lines], axis=0)
    far = jnp.concatenate(
        [line[96:144, 64 * h:64 * (h + 1)] for line in lines for h in range(2)], axis=0
    )
    return nn(regroup, jnp.concatenate([near, far], axis=1)).astype(BF)


def spread_out(part, charge, hosts, sector):
    lane = iota((1, 192), 1) // JB
    size = part.shape[0] // SEC
    rows = part[sector * size:(sector + 1) * size]
    for n in range(SEC):
        if not 0 <= sector + charge[ORDER[n]] < SEC:
            rows = jnp.where(lane == n, jnp.zeros((), BF), rows)
    host, spot = hosts[sector]
    return rows, part[host * size:(host + 1) * size, spot * JB:(spot + 1) * JB]


def mix_kernel(site, u, own, right, far, left, spread, left_q, image, moved, merged, mixed):
    regroup = regrouping(0, NX)
    left_q[...] = jnp.zeros(left_q.shape, BF)
    moved[...] = jnp.zeros(moved.shape, F32)
    for g in range(NY):
        part = regrouped(regroup, (own, right, far, left), g)
        for q in range(SEC):
            rows, last = spread_out(part, CHARGE, IN_PLACES, q)
            left_q[q, g * 48:(g + 1) * 48, 0:192] = rows
            left_q[q, g * 48:(g + 1) * 48, 192:216] = last
    for q in range(SEC):
        columns = u[:, q * JB:(q + 1) * JB, :].reshape(CAP, 128)
        image[q * 128:(q + 1) * 128, :] = tn(columns, left_q[q]).astype(BF)
    a, b = iota((256, 384), 0), iota((256, 384), 1)
    inside = b % 128
    order = one_hot((a == (inside // 8) * JB + (b // 128) * 8 + inside % 8) & (inside < 72))
    parted = nn(image[...], order)
    for q in range(SEC):
        for k in range(DD):
            p = q + CHARGE[k]
            if 0 <= p < SEC:
                rows = parted[q * 128 + k * XB:q * 128 + (k + 1) * XB]
                for part in range(3):
                    moved[part * 128 + p * XB:part * 128 + (p + 1) * XB, k * 128:(k + 1) * 128] = (
                        rows[:, part * 128:(part + 1) * 128]
                    )
    a, b = iota((81, DD * 128), 0), iota((81, DD * 128), 1)
    pos = (b % 128) // 8
    s = jnp.where(pos == 4, ORDER[4], jnp.where(pos == 5, ORDER[5], pos))
    a, b = iota((81, 81), 0), iota((81, 81), 1)
    even = charge_of(b // DD) + charge_of(a // DD) == charge_of(b % DD) + charge_of(a % DD)
    allowed = jnp.where(even, site[...], 0.0).astype(BF)
    a, b = iota((81, DD * 128), 0), iota((81, DD * 128), 1)
    wide = nn(allowed, one_hot((s + (b // 128) * DD == a) & (pos < DD)))
    a, b = iota((8, DD * 128), 0), iota((8, DD * 128), 1)
    same = (b % 8 == a) & (b % 128 < 72)
    weights = [
        jnp.where(same, wide[r * DD + l:r * DD + l + 1, :], 0.0) for r in ORDER for l in ORDER
    ]
    weights = jnp.concatenate(weights, axis=0).astype(BF)
    product = nt(weights, moved[...].astype(BF))
    for n in range(DD):
        for part in range(3):
            block = product[n * 72:(n + 1) * 72, part * 128:part * 128 + 96].reshape(DD, 8, 96)
            if n < SEC:
                merged[:, part, :, n * 96:(n + 1) * 96] = block
                continue
            for p, (host, spot) in enumerate(IN_PLACES):
                start = spot * 96 + host * XB
                merged[:, part, :, start:start + XB] = block[:, :, p * XB:(p + 1) * XB]
    mixed[0:216, :] = merged[...].reshape(216, SEC * 96).astype(BF)
    mixed[216:256, :] = jnp.zeros((40, SEC * 96), BF)
    lane = iota((1, SEC * 96), 1)
    sector = (lane % 96) // XB
    for n in range(SEC):
        sector = jnp.where(lane // 96 == n, sector + CHARGE[ORDER[n]], sector)
    for p, (host, spot) in enumerate(IN_PLACES):
        sector = jnp.where(lane // XB == spot * SEC + host, p, sector)
    for v in range(SEC):
        spread[v * 256:(v + 1) * 256, :] = jnp.where(sector == v, mixed[...], jnp.zeros((), BF))


def mix(site, u, pieces):
    return pl.pallas_call(
        mix_kernel,
        out_shape=jax.ShapeDtypeStruct((SEC * 256, SEC * 96), BF),
        in_specs=[VMEM] * 6,
        out_specs=VMEM,
        scratch_shapes=[
            pltpu.VMEM((SEC, CAP, 256), BF),
            pltpu.VMEM((SEC * 128, 256), BF),
            pltpu.VMEM((3 * 128, DD * 128), F32),
            pltpu.VMEM((DD, 3, 8, SEC * 96), F32),
            pltpu.VMEM((256, SEC * 96), BF),
        ],
        compiler_params=PARAMS,
        cost_estimate=pl.CostEstimate(flops=6_000_000_000, bytes_accessed=3_000_000, transcendentals=0),
        name="mix",
    )(site, u, *pieces)


def lower_kernel(half, spread, own, right, far, left, out, lower_v):
    regroup = regrouping(2 * lax.rem(lax.axis_index("lo") + half, 2), 2)
    lower_v[...] = jnp.zeros(lower_v.shape, BF)
    for g in range(NY):
        part = regrouped(regroup, (own, right, far, left), g)
        for v in range(SEC):
            rows, last = spread_out(part, [-c for c in CHARGE], OUT_PLACES, v)
            lower_v[g * JB:(g + 1) * JB, v * 256:v * 256 + 192] = rows
            lower_v[g * JB:(g + 1) * JB, v * 256 + 192:v * 256 + 216] = last
    for n in range(3):
        cut = slice(n * 256, (n + 1) * 256)
        total = nn(lower_v[...], spread[:, cut])
        out[:, :, cut] = total.reshape(NY, JB, 256).astype(out.dtype)


def contract_lower(half, spread, pieces):
    return pl.pallas_call(
        functools.partial(lower_kernel, half),
        out_shape=jax.ShapeDtypeStruct((NY, JB, SEC * 96), BF if half else F32),
        in_specs=[VMEM] * 5,
        out_specs=VMEM,
        scratch_shapes=[pltpu.VMEM((NY * JB, SEC * 256), BF)],
        compiler_params=PARAMS,
        cost_estimate=pl.CostEstimate(flops=3_000_000_000, bytes_accessed=3_000_000, transcendentals=0),
        name="lower_theirs" if half else "lower_ours",
    )(spread, *pieces)


def finish_kernel(terms, out, stacked):
    total = terms[0].astype(F32)
    for z in range(1, N_LO // 2):
        total = total + terms[z].astype(F32)
    for n in range(SEC):
        r = ORDER[n]
        stacked[r * JB:(r + 1) * JB, :] = total[:, n * 96:(n + 1) * 96]
    for p, (host, spot) in enumerate(IN_PLACES):
        start = spot * 96 + host * XB
        stacked[SEC * JB:DD * JB, p * XB:(p + 1) * XB] = total[:, start:start + XB]
    a, b = iota((96, 96), 0), iota((96, 96), 1)
    turned = nn(stacked[...].astype(BF), one_hot(b == (a % XB) * SEC + a // XB))
    p = iota((1, 96), 1) % SEC
    for r in range(DD):
        keep = (p + CHARGE[r] >= 0) & (p + CHARGE[r] < SEC)
        out[r] = jnp.where(keep, turned[r * JB:(r + 1) * JB, :], 0.0).astype(BF)


def finish(terms):
    return pl.pallas_call(
        finish_kernel,
        out_shape=jax.ShapeDtypeStruct((DD, JB, 96), BF),
        in_specs=[VMEM],
        out_specs=VMEM,
        scratch_shapes=[pltpu.VMEM((DD * JB, 96), F32)],
        compiler_params=PARAMS,
        name="finish",
    )(terms)


Z_GROUPS = [[2 * z + core for z in range(N_LO // 2)] for core in range(2)]
Y_GROUPS = [[y * NX + x for y in range(NY)] for x in range(NX)]


def from_x(value, d):
    pairs = [(y * NX + x, y * NX + (x - d) % NX) for y in range(NY) for x in range(NX)]
    return lax.ppermute(value, "up", pairs)


def local(sector_sizes, left, upper_edge, lower_edge, site_block):
    lb, u = prepare(sector_sizes, left, upper_edge, lower_edge)
    line = lax.all_to_all(lb, "up", 0, 0, axis_index_groups=Y_GROUPS)
    u = lax.all_gather(u, "lo", axis=0)
    line, u, site_block = lax.optimization_barrier((line, u, site_block))
    site = site_block.transpose(2, 3, 0, 1).reshape(81, 81)
    left, lower = line[:, 0], line[:, 1]
    left_right, left_left = from_x(left, 1), from_x(left, -1)
    lower_right, lower_left = from_x(lower, 1), from_x(lower, -1)
    left_far, lower_far = from_x(left_right, 1), from_x(lower_left, -1)
    spread = mix(site, u, (left, left_right, left_far, left_left))
    lines = (lower, lower_right, lower_far, lower_left)
    theirs = contract_lower(1, spread, lines)
    ours = contract_lower(0, spread, lines)
    swap = [(n, n + 1 - 2 * (n % 2)) for n in range(N_LO)]
    theirs = lax.ppermute(theirs, "lo", swap)
    terms = (ours + theirs.astype(F32)).astype(BF)
    terms = lax.all_to_all(terms, "lo", 0, 0, axis_index_groups=Z_GROUPS)
    return finish(terms)


def solution(mesh):
    return jax.shard_map(
        local,
        mesh=mesh,
        in_specs=(P(), P(None, "lo", "up"), P(None, "up", "lo"), P(None, "up", "lo"), P()),
        out_specs=P(None, "lo", "up"),
        check_vma=False,
    )
```

```python
import functools

import jax
import jax.numpy as jnp
from jax import lax
from jax.experimental import pallas as pl
from jax.experimental.pallas import tpu as pltpu
from jax.sharding import PartitionSpec as P

SEC = 8
DD = 9
NX = 4
NY = 8
N_UP = NX * NY
N_LO = 16
XB = 12
JB = 24
CAP = 384
CHARGE = [member // 3 - member % 3 for member in range(DD)]
ORDER = [0, 1, 2, 3, 5, 4, 6, 7, 8]


def places(charge):
    free = [(q, a) for q in range(SEC) for a in range(SEC) if not 0 <= q + charge[ORDER[a]] < SEC]
    found = [None] * SEC
    for q in range(SEC):
        own = [spot for spot in free if spot[0] == q]
        if own:
            found[q] = own[0]
            free.remove(own[0])
    for q in range(SEC):
        if found[q] is None:
            found[q] = free.pop(0)
    return found


IN_PLACES = places(CHARGE)
OUT_PLACES = places([-c for c in CHARGE])
BF = jnp.bfloat16
F32 = jnp.float32
VMEM = pl.BlockSpec(memory_space=pltpu.VMEM)
SMEM = pl.BlockSpec(memory_space=pltpu.SMEM)
PARAMS = pltpu.CompilerParams(vmem_limit_bytes=16 * 1024 * 1024)
WIDE = pltpu.CompilerParams(vmem_limit_bytes=56 * 1024 * 1024)


def nt(a, b):
    return lax.dot_general(a, b, (((1,), (1,)), ((), ())), preferred_element_type=F32)


def nn(a, b):
    return lax.dot_general(a, b, (((1,), (0,)), ((), ())), preferred_element_type=F32)


def tn(a, b):
    return lax.dot_general(a, b, (((0,), (0,)), ((), ())), preferred_element_type=F32)


def iota(shape, axis):
    return lax.broadcasted_iota(jnp.int32, shape, axis)


def one_hot(flag):
    return jnp.where(flag, 1.0, 0.0).astype(BF)


def sizes_by_sector(sizes_ref, sector, charge):
    found = jnp.zeros(sector.shape, jnp.int32)
    for q in range(SEC):
        if 0 <= q + charge < SEC:
            found = jnp.where(sector == q, sizes_ref[q + charge], found)
    return found


def prepare_kernel(sizes, left, upper, lower, lb_out, u_out, left_s, up_s, wide_s, pack):
    up, lo = lax.axis_index("up"), lax.axis_index("lo")
    lane = iota((1, XB * SEC), 1)
    live = up * XB + lane // SEC < sizes_by_sector(sizes, lane % SEC, 0)
    row = lo * JB + iota((JB, 1), 0)
    limit = {c: sizes_by_sector(sizes, lane % SEC, c) for c in sorted(set(CHARGE))}
    for a, s in enumerate(ORDER):
        keep = live & (row < limit[CHARGE[s]])
        left_s[a * JB:(a + 1) * JB, :] = jnp.where(keep, left[s].astype(F32), 0.0)
    a, b = iota((96, 96), 0), iota((96, 96), 1)
    order = one_hot(b == (a % XB) * SEC + a // XB)
    grid = nt(order, left_s[...].astype(BF))
    pack[0] = grid[:, 0:192]
    for q, (host, at) in enumerate(IN_PLACES):
        pack[0, host * XB:(host + 1) * XB, at * JB:(at + 1) * JB] = grid[q * XB:(q + 1) * XB, 192:216]
    lane = iota((1, JB * SEC), 1)
    live = lo * JB + lane // SEC < sizes_by_sector(sizes, lane % SEC, 0)
    row = up * XB + iota((XB, 1), 0)
    limit = {c: sizes_by_sector(sizes, lane % SEC, c) for c in sorted(set(CHARGE))}
    blank = jnp.zeros((4, JB * SEC), F32)
    for k in range(DD):
        keep = live & (row < limit[CHARGE[k]])
        up_s[0, k * 16:k * 16 + XB, :] = jnp.where(keep, upper[k].astype(F32), 0.0)
        up_s[0, k * 16 + XB:(k + 1) * 16, :] = blank
        up_s[1, k * 16:k * 16 + XB, :] = jnp.where(keep, lower[k].astype(F32), 0.0)
        up_s[1, k * 16 + XB:(k + 1) * 16, :] = blank
    a, b = iota((128, 144), 0), iota((128, 144), 1)
    dense = nn(one_hot((b == (a // XB) * 16 + a % XB) & (a < 108)), up_s[0].astype(BF)).astype(BF)
    a, b = iota((192, 192), 0), iota((192, 192), 1)
    edge = nt(one_hot(b == (a % JB) * SEC + a // JB), dense).astype(BF)
    a, b = iota((DD * 96, 144), 0), iota((DD * 96, 144), 1)
    pos = a // 96
    l = jnp.where(pos == 4, ORDER[4], jnp.where(pos == 5, ORDER[5], pos))
    copies = nn(one_hot(b == l * 16 + a % XB), up_s[1].astype(BF))
    sector = iota((96, 192), 0) // XB - iota((96, 192), 1) % SEC
    for n, l in enumerate(ORDER):
        wide_s[n * 96:(n + 1) * 96, :] = jnp.where(
            sector == CHARGE[l], copies[n * 96:(n + 1) * 96], 0.0
        ).astype(BF)
    a, b = iota((192, 128), 0), iota((192, 128), 1)
    folded = nn(wide_s[...], one_hot(b == a // SEC))
    for n in range(SEC):
        pack[1, :, n * JB:(n + 1) * JB] = folded[n * 96:(n + 1) * 96, 0:JB]
    for v, (host, at) in enumerate(OUT_PLACES):
        row = SEC * 96 + v * XB
        pack[1, host * XB:(host + 1) * XB, at * JB:(at + 1) * JB] = folded[row:row + XB, 0:JB]
    for n in range(NY):
        for side in range(2):
            lb_out[n, side, 0:96, :] = pack[side, :, 0:128].astype(BF)
            lb_out[n, side, 96:144, 0:64] = pack[side, 0:48, 128:192].astype(BF)
            lb_out[n, side, 96:144, 64:128] = pack[side, 48:96, 128:192].astype(BF)
    u_out[...] = edge


def prepare(sizes, left, upper, lower):
    return pl.pallas_call(
        prepare_kernel,
        out_shape=(
            jax.ShapeDtypeStruct((NY, 2, 144, 128), BF),
            jax.ShapeDtypeStruct((192, 128), BF),
        ),
        in_specs=[SMEM, VMEM, VMEM, VMEM],
        out_specs=(VMEM, VMEM),
        scratch_shapes=[
            pltpu.VMEM((216, 96), F32),
            pltpu.VMEM((2, 144, 192), F32),
            pltpu.VMEM((DD * 96, 192), BF),
            pltpu.VMEM((2, 96, 192), F32),
        ],
        compiler_params=WIDE,
        name="prepare",
    )(sizes, left, upper, lower)


def charge_of(member):
    return member // 3 - member % 3


def regrouping(turn, count):
    a, b = iota((count * 96, 384), 0), iota((count * 96, 384), 1)
    size = count * XB
    d = ((a % size) // XB + turn + NX - lax.axis_index("up") % NX) % NX
    return one_hot(b == d * 96 + (a // size) * XB + a % XB)


def regrouped(regroup, pieces, g):
    lines = [piece[g] for piece in pieces]
    near = jnp.concatenate([line[0:96, :] for line in lines], axis=0)
    far = jnp.concatenate(
        [line[96:144, 64 * h:64 * (h + 1)] for line in lines for h in range(2)], axis=0
    )
    return nn(regroup, jnp.concatenate([near, far], axis=1)).astype(BF)


def spread_out(part, charge, hosts, sector):
    lane = iota((1, 192), 1) // JB
    size = part.shape[0] // SEC
    rows = part[sector * size:(sector + 1) * size]
    for n in range(SEC):
        if not 0 <= sector + charge[ORDER[n]] < SEC:
            rows = jnp.where(lane == n, jnp.zeros((), BF), rows)
    host, spot = hosts[sector]
    return rows, part[host * size:(host + 1) * size, spot * JB:(spot + 1) * JB]


def mix_kernel(site, u, own, right, far, left, spread, left_q, image, moved, merged, mixed, legs):
    regroup = regrouping(0, NX)
    left_q[...] = jnp.zeros(left_q.shape, BF)
    moved[...] = jnp.zeros(moved.shape, F32)
    for g in range(NY):
        part = regrouped(regroup, (own, right, far, left), g)
        for q in range(SEC):
            rows, last = spread_out(part, CHARGE, IN_PLACES, q)
            left_q[q, g * 48:(g + 1) * 48, 0:192] = rows
            left_q[q, g * 48:(g + 1) * 48, 192:216] = last
    for q in range(SEC):
        columns = u[:, q * JB:(q + 1) * JB, :].reshape(CAP, 128)
        image[q * 128:(q + 1) * 128, :] = tn(columns, left_q[q]).astype(BF)
    a, b = iota((256, 384), 0), iota((256, 384), 1)
    inside = b % 128
    order = one_hot((a == (inside // 8) * JB + (b // 128) * 8 + inside % 8) & (inside < 72))
    parted = nn(image[...], order)
    for q in range(SEC):
        for k in range(DD):
            p = q + CHARGE[k]
            if 0 <= p < SEC:
                rows = parted[q * 128 + k * XB:q * 128 + (k + 1) * XB]
                for part in range(3):
                    moved[part * 128 + p * XB:part * 128 + (p + 1) * XB, k * 128:(k + 1) * 128] = (
                        rows[:, part * 128:(part + 1) * 128]
                    )
    for n in range(DD * DD):
        legs[n * 16:n * 16 + DD, 0:DD] = site[n // DD, n % DD]
    a, b = iota((81, DD * 128), 0), iota((81, DD * 128), 1)
    pos = (b % 128) // 8
    s = jnp.where(pos == 4, ORDER[4], jnp.where(pos == 5, ORDER[5], pos))
    widen = one_hot((s + (b // 128) * DD == a) & (pos < DD))
    l, b = iota((16, DD * 128), 0), iota((16, DD * 128), 1)
    pos = (b % 128) // 8
    s = jnp.where(pos == 4, ORDER[4], jnp.where(pos == 5, ORDER[5], pos))
    balance = charge_of(b // 128) - charge_of(s) - charge_of(l)
    wide = []
    for r in range(DD):
        rows = tn(legs[pl.ds(r, DD * DD, stride=16), :].astype(BF), widen)[0:16]
        wide.append(jnp.where(balance == -CHARGE[r], rows, 0.0))
    a, b = iota((8, DD * 128), 0), iota((8, DD * 128), 1)
    same = (b % 8 == a) & (b % 128 < 72)
    weights = [
        jnp.where(same, wide[r][l:l + 1, :], 0.0) for r in ORDER for l in ORDER
    ]
    weights = jnp.concatenate(weights, axis=0).astype(BF)
    product = nt(weights, moved[...].astype(BF))
    for n in range(DD):
        for part in range(3):
            block = product[n * 72:(n + 1) * 72, part * 128:part * 128 + 96].reshape(DD, 8, 96)
            if n < SEC:
                merged[:, part, :, n * 96:(n + 1) * 96] = block
                continue
            for p, (host, spot) in enumerate(IN_PLACES):
                start = spot * 96 + host * XB
                merged[:, part, :, start:start + XB] = block[:, :, p * XB:(p + 1) * XB]
    mixed[0:216, :] = merged[...].reshape(216, SEC * 96).astype(BF)
    mixed[216:256, :] = jnp.zeros((40, SEC * 96), BF)
    lane = iota((1, SEC * 96), 1)
    sector = (lane % 96) // XB
    for n in range(SEC):
        sector = jnp.where(lane // 96 == n, sector + CHARGE[ORDER[n]], sector)
    for p, (host, spot) in enumerate(IN_PLACES):
        sector = jnp.where(lane // XB == spot * SEC + host, p, sector)
    for v in range(SEC):
        spread[v * 256:(v + 1) * 256, :] = jnp.where(sector == v, mixed[...], jnp.zeros((), BF))


def mix(site, u, pieces):
    return pl.pallas_call(
        mix_kernel,
        out_shape=jax.ShapeDtypeStruct((SEC * 256, SEC * 96), BF),
        in_specs=[VMEM] * 6,
        out_specs=VMEM,
        scratch_shapes=[
            pltpu.VMEM((SEC, CAP, 256), BF),
            pltpu.VMEM((SEC * 128, 256), BF),
            pltpu.VMEM((3 * 128, DD * 128), F32),
            pltpu.VMEM((DD, 3, 8, SEC * 96), F32),
            pltpu.VMEM((256, SEC * 96), BF),
            pltpu.VMEM((DD * DD * 16, 128), F32),
        ],
        compiler_params=PARAMS,
        cost_estimate=pl.CostEstimate(flops=6_000_000_000, bytes_accessed=3_000_000, transcendentals=0),
        name="mix",
    )(site, u, *pieces)


def lower_kernel(half, spread, own, right, far, left, out, lower_v):
    regroup = regrouping(2 * lax.rem(lax.axis_index("lo") + half, 2), 2)
    lower_v[...] = jnp.zeros(lower_v.shape, BF)
    for g in range(NY):
        part = regrouped(regroup, (own, right, far, left), g)
        for v in range(SEC):
            rows, last = spread_out(part, [-c for c in CHARGE], OUT_PLACES, v)
            lower_v[g * JB:(g + 1) * JB, v * 256:v * 256 + 192] = rows
            lower_v[g * JB:(g + 1) * JB, v * 256 + 192:v * 256 + 216] = last
    for n in range(3):
        cut = slice(n * 256, (n + 1) * 256)
        total = nn(lower_v[...], spread[:, cut])
        out[:, :, cut] = total.reshape(NY, JB, 256).astype(out.dtype)


def contract_lower(half, spread, pieces):
    return pl.pallas_call(
        functools.partial(lower_kernel, half),
        out_shape=jax.ShapeDtypeStruct((NY, JB, SEC * 96), BF if half else F32),
        in_specs=[VMEM] * 5,
        out_specs=VMEM,
        scratch_shapes=[pltpu.VMEM((NY * JB, SEC * 256), BF)],
        compiler_params=PARAMS,
        cost_estimate=pl.CostEstimate(flops=3_000_000_000, bytes_accessed=3_000_000, transcendentals=0),
        name="lower_theirs" if half else "lower_ours",
    )(spread, *pieces)


def finish_kernel(terms, out, stacked):
    total = terms[0].astype(F32)
    for z in range(1, N_LO // 2):
        total = total + terms[z].astype(F32)
    for n in range(SEC):
        r = ORDER[n]
        stacked[r * JB:(r + 1) * JB, :] = total[:, n * 96:(n + 1) * 96]
    for p, (host, spot) in enumerate(IN_PLACES):
        start = spot * 96 + host * XB
        stacked[SEC * JB:DD * JB, p * XB:(p + 1) * XB] = total[:, start:start + XB]
    a, b = iota((96, 96), 0), iota((96, 96), 1)
    turned = nn(stacked[...].astype(BF), one_hot(b == (a % XB) * SEC + a // XB))
    p = iota((1, 96), 1) % SEC
    for r in range(DD):
        keep = (p + CHARGE[r] >= 0) & (p + CHARGE[r] < SEC)
        out[r] = jnp.where(keep, turned[r * JB:(r + 1) * JB, :], 0.0).astype(BF)


def finish(terms):
    return pl.pallas_call(
        finish_kernel,
        out_shape=jax.ShapeDtypeStruct((DD, JB, 96), BF),
        in_specs=[VMEM],
        out_specs=VMEM,
        scratch_shapes=[pltpu.VMEM((DD * JB, 96), F32)],
        compiler_params=PARAMS,
        name="finish",
    )(terms)


Z_GROUPS = [[2 * z + core for z in range(N_LO // 2)] for core in range(2)]
Y_GROUPS = [[y * NX + x for y in range(NY)] for x in range(NX)]


def from_x(value, d):
    pairs = [(y * NX + x, y * NX + (x - d) % NX) for y in range(NY) for x in range(NX)]
    return lax.ppermute(value, "up", pairs)


def local(sector_sizes, left, upper_edge, lower_edge, site_block):
    lb, u = prepare(sector_sizes, left, upper_edge, lower_edge)
    line = lax.all_to_all(lb, "up", 0, 0, axis_index_groups=Y_GROUPS)
    u = lax.all_gather(u, "lo", axis=0)
    line, u = lax.optimization_barrier((line, u))
    left, lower = line[:, 0], line[:, 1]
    left_right, left_left = from_x(left, 1), from_x(left, -1)
    lower_right, lower_left = from_x(lower, 1), from_x(lower, -1)
    left_far, lower_far = from_x(left_right, 1), from_x(lower_left, -1)
    spread = mix(site_block, u, (left, left_right, left_far, left_left))
    lines = (lower, lower_right, lower_far, lower_left)
    theirs = contract_lower(1, spread, lines)
    ours = contract_lower(0, spread, lines)
    swap = [(n, n + 1 - 2 * (n % 2)) for n in range(N_LO)]
    theirs = lax.ppermute(theirs, "lo", swap)
    terms = (ours + theirs.astype(F32)).astype(BF)
    terms = lax.all_to_all(terms, "lo", 0, 0, axis_index_groups=Z_GROUPS)
    return finish(terms)


def solution(mesh):
    return jax.shard_map(
        local,
        mesh=mesh,
        in_specs=(P(), P(None, "lo", "up"), P(None, "up", "lo"), P(None, "up", "lo"), P()),
        out_specs=P(None, "lo", "up"),
        check_vma=False,
    )
```

```python
import functools

import jax
import jax.numpy as jnp
from jax import lax
from jax.experimental import pallas as pl
from jax.experimental.pallas import tpu as pltpu
from jax.sharding import PartitionSpec as P

SEC = 8
DD = 9
NX = 4
NY = 8
N_UP = NX * NY
N_LO = 16
XB = 12
JB = 24
CAP = 384
CHARGE = [member // 3 - member % 3 for member in range(DD)]
ORDER = [0, 1, 2, 3, 5, 4, 6, 7, 8]


def places(charge):
    free = [(q, a) for q in range(SEC) for a in range(SEC) if not 0 <= q + charge[ORDER[a]] < SEC]
    found = [None] * SEC
    for q in range(SEC):
        own = [spot for spot in free if spot[0] == q]
        if own:
            found[q] = own[0]
            free.remove(own[0])
    for q in range(SEC):
        if found[q] is None:
            found[q] = free.pop(0)
    return found


IN_PLACES = places(CHARGE)
OUT_PLACES = places([-c for c in CHARGE])
BF = jnp.bfloat16
F32 = jnp.float32
VMEM = pl.BlockSpec(memory_space=pltpu.VMEM)
SMEM = pl.BlockSpec(memory_space=pltpu.SMEM)
PARAMS = pltpu.CompilerParams(vmem_limit_bytes=16 * 1024 * 1024)
WIDE = pltpu.CompilerParams(vmem_limit_bytes=56 * 1024 * 1024)


def nt(a, b):
    return lax.dot_general(a, b, (((1,), (1,)), ((), ())), preferred_element_type=F32)


def nn(a, b):
    return lax.dot_general(a, b, (((1,), (0,)), ((), ())), preferred_element_type=F32)


def tn(a, b):
    return lax.dot_general(a, b, (((0,), (0,)), ((), ())), preferred_element_type=F32)


def iota(shape, axis):
    return lax.broadcasted_iota(jnp.int32, shape, axis)


def one_hot(flag):
    return jnp.where(flag, 1.0, 0.0).astype(BF)


def sizes_by_sector(sizes_ref, sector, charge):
    found = jnp.zeros(sector.shape, jnp.int32)
    for q in range(SEC):
        if 0 <= q + charge < SEC:
            found = jnp.where(sector == q, sizes_ref[q + charge], found)
    return found


def prepare_kernel(sizes, left, upper, lower, lb_out, u_out, left_s, up_s, wide_s, pack):
    up, lo = lax.axis_index("up"), lax.axis_index("lo")
    lane = iota((1, XB * SEC), 1)
    live = up * XB + lane // SEC < sizes_by_sector(sizes, lane % SEC, 0)
    row = lo * JB + iota((JB, 1), 0)
    limit = {c: sizes_by_sector(sizes, lane % SEC, c) for c in sorted(set(CHARGE))}
    for a, s in enumerate(ORDER):
        keep = live & (row < limit[CHARGE[s]])
        left_s[a * JB:(a + 1) * JB, :] = jnp.where(keep, left[s].astype(F32), 0.0)
    a, b = iota((96, 96), 0), iota((96, 96), 1)
    order = one_hot(b == (a % XB) * SEC + a // XB)
    grid = nt(order, left_s[...].astype(BF))
    pack[0] = grid[:, 0:192]
    for q, (host, at) in enumerate(IN_PLACES):
        pack[0, host * XB:(host + 1) * XB, at * JB:(at + 1) * JB] = grid[q * XB:(q + 1) * XB, 192:216]
    lane = iota((1, JB * SEC), 1)
    live = lo * JB + lane // SEC < sizes_by_sector(sizes, lane % SEC, 0)
    row = up * XB + iota((XB, 1), 0)
    limit = {c: sizes_by_sector(sizes, lane % SEC, c) for c in sorted(set(CHARGE))}
    blank = jnp.zeros((4, JB * SEC), F32)
    for k in range(DD):
        keep = live & (row < limit[CHARGE[k]])
        up_s[0, k * 16:k * 16 + XB, :] = jnp.where(keep, upper[k].astype(F32), 0.0)
        up_s[0, k * 16 + XB:(k + 1) * 16, :] = blank
        up_s[1, k * 16:k * 16 + XB, :] = jnp.where(keep, lower[k].astype(F32), 0.0)
        up_s[1, k * 16 + XB:(k + 1) * 16, :] = blank
    a, b = iota((128, 144), 0), iota((128, 144), 1)
    dense = nn(one_hot((b == (a // XB) * 16 + a % XB) & (a < 108)), up_s[0].astype(BF)).astype(BF)
    a, b = iota((192, 192), 0), iota((192, 192), 1)
    edge = nt(one_hot(b == (a % JB) * SEC + a // JB), dense).astype(BF)
    a, b = iota((DD * 96, 144), 0), iota((DD * 96, 144), 1)
    pos = a // 96
    l = jnp.where(pos == 4, ORDER[4], jnp.where(pos == 5, ORDER[5], pos))
    copies = nn(one_hot(b == l * 16 + a % XB), up_s[1].astype(BF))
    sector = iota((96, 192), 0) // XB - iota((96, 192), 1) % SEC
    for n, l in enumerate(ORDER):
        wide_s[n * 96:(n + 1) * 96, :] = jnp.where(
            sector == CHARGE[l], copies[n * 96:(n + 1) * 96], 0.0
        ).astype(BF)
    a, b = iota((192, 128), 0), iota((192, 128), 1)
    folded = nn(wide_s[...], one_hot(b == a // SEC))
    for n in range(SEC):
        pack[1, :, n * JB:(n + 1) * JB] = folded[n * 96:(n + 1) * 96, 0:JB]
    for v, (host, at) in enumerate(OUT_PLACES):
        row = SEC * 96 + v * XB
        pack[1, host * XB:(host + 1) * XB, at * JB:(at + 1) * JB] = folded[row:row + XB, 0:JB]
    for n in range(NY):
        for side in range(2):
            lb_out[n, side, 0:96, :] = pack[side, :, 0:128].astype(BF)
            lb_out[n, side, 96:144, 0:64] = pack[side, 0:48, 128:192].astype(BF)
            lb_out[n, side, 96:144, 64:128] = pack[side, 48:96, 128:192].astype(BF)
    u_out[...] = edge


def prepare(sizes, left, upper, lower):
    return pl.pallas_call(
        prepare_kernel,
        out_shape=(
            jax.ShapeDtypeStruct((NY, 2, 144, 128), BF),
            jax.ShapeDtypeStruct((192, 128), BF),
        ),
        in_specs=[SMEM, VMEM, VMEM, VMEM],
        out_specs=(VMEM, VMEM),
        scratch_shapes=[
            pltpu.VMEM((216, 96), F32),
            pltpu.VMEM((2, 144, 192), F32),
            pltpu.VMEM((DD * 96, 192), BF),
            pltpu.VMEM((2, 96, 192), F32),
        ],
        compiler_params=WIDE,
        name="prepare",
    )(sizes, left, upper, lower)


def charge_of(member):
    return member // 3 - member % 3


def regrouping(turn, count):
    a, b = iota((count * 96, 384), 0), iota((count * 96, 384), 1)
    size = count * XB
    d = ((a % size) // XB + turn + NX - lax.axis_index("up") % NX) % NX
    return one_hot(b == d * 96 + (a // size) * XB + a % XB)


def regrouped(regroup, pieces, g):
    lines = [piece[g] for piece in pieces]
    near = jnp.concatenate([line[0:96, :] for line in lines], axis=0)
    far = jnp.concatenate(
        [line[96:144, 64 * h:64 * (h + 1)] for line in lines for h in range(2)], axis=0
    )
    return nn(regroup, jnp.concatenate([near, far], axis=1)).astype(BF)


def spread_out(part, charge, hosts, sector):
    lane = iota((1, 192), 1) // JB
    size = part.shape[0] // SEC
    rows = part[sector * size:(sector + 1) * size]
    for n in range(SEC):
        if not 0 <= sector + charge[ORDER[n]] < SEC:
            rows = jnp.where(lane == n, jnp.zeros((), BF), rows)
    host, spot = hosts[sector]
    return rows, part[host * size:(host + 1) * size, spot * JB:(spot + 1) * JB]


def mix_kernel(site, u, own, right, far, left, spread, left_q, image, moved, merged, mixed, legs):
    regroup = regrouping(0, NX)
    left_q[...] = jnp.zeros(left_q.shape, BF)
    moved[...] = jnp.zeros(moved.shape, F32)
    for g in range(NY):
        part = regrouped(regroup, (own, right, far, left), g)
        for q in range(SEC):
            rows, last = spread_out(part, CHARGE, IN_PLACES, q)
            left_q[q, g * 48:(g + 1) * 48, 0:192] = rows
            left_q[q, g * 48:(g + 1) * 48, 192:216] = last
    for q in range(SEC):
        columns = u[:, q * JB:(q + 1) * JB, :].reshape(CAP, 128)
        image[q * 128:(q + 1) * 128, :] = tn(columns, left_q[q]).astype(BF)
    a, b = iota((256, 384), 0), iota((256, 384), 1)
    inside = b % 128
    order = one_hot((a == (inside // 8) * JB + (b // 128) * 8 + inside % 8) & (inside < 72))
    parted = nn(image[...], order)
    for q in range(SEC):
        for k in range(DD):
            p = q + CHARGE[k]
            if 0 <= p < SEC:
                rows = parted[q * 128 + k * XB:q * 128 + (k + 1) * XB]
                for part in range(3):
                    moved[part * 128 + p * XB:part * 128 + (p + 1) * XB, k * 128:(k + 1) * 128] = (
                        rows[:, part * 128:(part + 1) * 128]
                    )
    legs[...] = jnp.zeros(legs.shape, F32)
    for n in range(DD * DD):
        legs[n * 16:n * 16 + DD, 0:DD] = site[n // DD, n % DD]
    a, b = iota((88, DD * 128), 0), iota((88, DD * 128), 1)
    pos = (b % 128) // 8
    s = jnp.where(pos == 4, ORDER[4], jnp.where(pos == 5, ORDER[5], pos))
    widen = one_hot((s + (b // 128) * DD == a) & (pos < DD))
    l, b = iota((16, DD * 128), 0), iota((16, DD * 128), 1)
    pos = (b % 128) // 8
    s = jnp.where(pos == 4, ORDER[4], jnp.where(pos == 5, ORDER[5], pos))
    balance = charge_of(b // 128) - charge_of(s) - charge_of(l)
    wide = []
    for r in range(DD):
        rows = tn(legs[pl.ds(r, 88, stride=16), :].astype(BF), widen)[0:16]
        wide.append(jnp.where(balance == -CHARGE[r], rows, 0.0))
    a, b = iota((8, DD * 128), 0), iota((8, DD * 128), 1)
    same = (b % 8 == a) & (b % 128 < 72)
    weights = [
        jnp.where(same, wide[r][l:l + 1, :], 0.0) for r in ORDER for l in ORDER
    ]
    weights = jnp.concatenate(weights, axis=0).astype(BF)
    product = nt(weights, moved[...].astype(BF))
    for n in range(DD):
        for part in range(3):
            block = product[n * 72:(n + 1) * 72, part * 128:part * 128 + 96].reshape(DD, 8, 96)
            if n < SEC:
                merged[:, part, :, n * 96:(n + 1) * 96] = block
                continue
            for p, (host, spot) in enumerate(IN_PLACES):
                start = spot * 96 + host * XB
                merged[:, part, :, start:start + XB] = block[:, :, p * XB:(p + 1) * XB]
    mixed[0:216, :] = merged[...].reshape(216, SEC * 96).astype(BF)
    mixed[216:256, :] = jnp.zeros((40, SEC * 96), BF)
    lane = iota((1, SEC * 96), 1)
    sector = (lane % 96) // XB
    for n in range(SEC):
        sector = jnp.where(lane // 96 == n, sector + CHARGE[ORDER[n]], sector)
    for p, (host, spot) in enumerate(IN_PLACES):
        sector = jnp.where(lane // XB == spot * SEC + host, p, sector)
    for v in range(SEC):
        spread[v * 256:(v + 1) * 256, :] = jnp.where(sector == v, mixed[...], jnp.zeros((), BF))


def mix(site, u, pieces):
    return pl.pallas_call(
        mix_kernel,
        out_shape=jax.ShapeDtypeStruct((SEC * 256, SEC * 96), BF),
        in_specs=[VMEM] * 6,
        out_specs=VMEM,
        scratch_shapes=[
            pltpu.VMEM((SEC, CAP, 256), BF),
            pltpu.VMEM((SEC * 128, 256), BF),
            pltpu.VMEM((3 * 128, DD * 128), F32),
            pltpu.VMEM((DD, 3, 8, SEC * 96), F32),
            pltpu.VMEM((256, SEC * 96), BF),
            pltpu.VMEM((89 * 16, 128), F32),
        ],
        compiler_params=PARAMS,
        cost_estimate=pl.CostEstimate(flops=6_000_000_000, bytes_accessed=3_000_000, transcendentals=0),
        name="mix",
    )(site, u, *pieces)


def lower_kernel(half, spread, own, right, far, left, out, lower_v):
    regroup = regrouping(2 * lax.rem(lax.axis_index("lo") + half, 2), 2)
    lower_v[...] = jnp.zeros(lower_v.shape, BF)
    for g in range(NY):
        part = regrouped(regroup, (own, right, far, left), g)
        for v in range(SEC):
            rows, last = spread_out(part, [-c for c in CHARGE], OUT_PLACES, v)
            lower_v[g * JB:(g + 1) * JB, v * 256:v * 256 + 192] = rows
            lower_v[g * JB:(g + 1) * JB, v * 256 + 192:v * 256 + 216] = last
    for n in range(3):
        cut = slice(n * 256, (n + 1) * 256)
        total = nn(lower_v[...], spread[:, cut])
        out[:, :, cut] = total.reshape(NY, JB, 256).astype(out.dtype)


def contract_lower(half, spread, pieces):
    return pl.pallas_call(
        functools.partial(lower_kernel, half),
        out_shape=jax.ShapeDtypeStruct((NY, JB, SEC * 96), BF if half else F32),
        in_specs=[VMEM] * 5,
        out_specs=VMEM,
        scratch_shapes=[pltpu.VMEM((NY * JB, SEC * 256), BF)],
        compiler_params=PARAMS,
        cost_estimate=pl.CostEstimate(flops=3_000_000_000, bytes_accessed=3_000_000, transcendentals=0),
        name="lower_theirs" if half else "lower_ours",
    )(spread, *pieces)


def finish_kernel(terms, out, stacked):
    total = terms[0].astype(F32)
    for z in range(1, N_LO // 2):
        total = total + terms[z].astype(F32)
    for n in range(SEC):
        r = ORDER[n]
        stacked[r * JB:(r + 1) * JB, :] = total[:, n * 96:(n + 1) * 96]
    for p, (host, spot) in enumerate(IN_PLACES):
        start = spot * 96 + host * XB
        stacked[SEC * JB:DD * JB, p * XB:(p + 1) * XB] = total[:, start:start + XB]
    a, b = iota((96, 96), 0), iota((96, 96), 1)
    turned = nn(stacked[...].astype(BF), one_hot(b == (a % XB) * SEC + a // XB))
    p = iota((1, 96), 1) % SEC
    for r in range(DD):
        keep = (p + CHARGE[r] >= 0) & (p + CHARGE[r] < SEC)
        out[r] = jnp.where(keep, turned[r * JB:(r + 1) * JB, :], 0.0).astype(BF)


def finish(terms):
    return pl.pallas_call(
        finish_kernel,
        out_shape=jax.ShapeDtypeStruct((DD, JB, 96), BF),
        in_specs=[VMEM],
        out_specs=VMEM,
        scratch_shapes=[pltpu.VMEM((DD * JB, 96), F32)],
        compiler_params=PARAMS,
        name="finish",
    )(terms)


Z_GROUPS = [[2 * z + core for z in range(N_LO // 2)] for core in range(2)]
Y_GROUPS = [[y * NX + x for y in range(NY)] for x in range(NX)]


def from_x(value, d):
    pairs = [(y * NX + x, y * NX + (x - d) % NX) for y in range(NY) for x in range(NX)]
    return lax.ppermute(value, "up", pairs)


def local(sector_sizes, left, upper_edge, lower_edge, site_block):
    lb, u = prepare(sector_sizes, left, upper_edge, lower_edge)
    line = lax.all_to_all(lb, "up", 0, 0, axis_index_groups=Y_GROUPS)
    u = lax.all_gather(u, "lo", axis=0)
    line, u = lax.optimization_barrier((line, u))
    left, lower = line[:, 0], line[:, 1]
    left_right, left_left = from_x(left, 1), from_x(left, -1)
    lower_right, lower_left = from_x(lower, 1), from_x(lower, -1)
    left_far, lower_far = from_x(left_right, 1), from_x(lower_left, -1)
    spread = mix(site_block, u, (left, left_right, left_far, left_left))
    lines = (lower, lower_right, lower_far, lower_left)
    theirs = contract_lower(1, spread, lines)
    ours = contract_lower(0, spread, lines)
    swap = [(n, n + 1 - 2 * (n % 2)) for n in range(N_LO)]
    theirs = lax.ppermute(theirs, "lo", swap)
    terms = (ours + theirs.astype(F32)).astype(BF)
    terms = lax.all_to_all(terms, "lo", 0, 0, axis_index_groups=Z_GROUPS)
    return finish(terms)


def solution(mesh):
    return jax.shard_map(
        local,
        mesh=mesh,
        in_specs=(P(), P(None, "lo", "up"), P(None, "up", "lo"), P(None, "up", "lo"), P()),
        out_specs=P(None, "lo", "up"),
        check_vma=False,
    )
```

```python
import functools

import jax
import jax.numpy as jnp
from jax import lax
from jax.experimental import pallas as pl
from jax.experimental.pallas import tpu as pltpu
from jax.sharding import PartitionSpec as P

SEC = 8
DD = 9
NX = 4
NY = 8
N_UP = NX * NY
N_LO = 16
XB = 12
JB = 24
CAP = 384
CHARGE = [member // 3 - member % 3 for member in range(DD)]
ORDER = [0, 1, 2, 3, 5, 4, 6, 7, 8]


def places(charge):
    free = [(q, a) for q in range(SEC) for a in range(SEC) if not 0 <= q + charge[ORDER[a]] < SEC]
    found = [None] * SEC
    for q in range(SEC):
        own = [spot for spot in free if spot[0] == q]
        if own:
            found[q] = own[0]
            free.remove(own[0])
    for q in range(SEC):
        if found[q] is None:
            found[q] = free.pop(0)
    return found


IN_PLACES = places(CHARGE)
OUT_PLACES = places([-c for c in CHARGE])
BF = jnp.bfloat16
F32 = jnp.float32
VMEM = pl.BlockSpec(memory_space=pltpu.VMEM)
SMEM = pl.BlockSpec(memory_space=pltpu.SMEM)
PARAMS = pltpu.CompilerParams(vmem_limit_bytes=16 * 1024 * 1024)
WIDE = pltpu.CompilerParams(vmem_limit_bytes=56 * 1024 * 1024)


def nt(a, b):
    return lax.dot_general(a, b, (((1,), (1,)), ((), ())), preferred_element_type=F32)


def nn(a, b):
    return lax.dot_general(a, b, (((1,), (0,)), ((), ())), preferred_element_type=F32)


def tn(a, b):
    return lax.dot_general(a, b, (((0,), (0,)), ((), ())), preferred_element_type=F32)


def iota(shape, axis):
    return lax.broadcasted_iota(jnp.int32, shape, axis)


def one_hot(flag):
    return jnp.where(flag, 1.0, 0.0).astype(BF)


def sizes_by_sector(sizes_ref, sector, charge):
    found = jnp.zeros(sector.shape, jnp.int32)
    for q in range(SEC):
        if 0 <= q + charge < SEC:
            found = jnp.where(sector == q, sizes_ref[q + charge], found)
    return found


def prepare_kernel(sizes, left, upper, lower, lb_out, u_out, left_s, up_s, wide_s, pack):
    up, lo = lax.axis_index("up"), lax.axis_index("lo")
    lane = iota((1, XB * SEC), 1)
    live = up * XB + lane // SEC < sizes_by_sector(sizes, lane % SEC, 0)
    row = lo * JB + iota((JB, 1), 0)
    limit = {c: sizes_by_sector(sizes, lane % SEC, c) for c in sorted(set(CHARGE))}
    for a, s in enumerate(ORDER):
        keep = live & (row < limit[CHARGE[s]])
        left_s[a * JB:(a + 1) * JB, :] = jnp.where(keep, left[s].astype(F32), 0.0)
    a, b = iota((96, 96), 0), iota((96, 96), 1)
    order = one_hot(b == (a % XB) * SEC + a // XB)
    grid = nt(order, left_s[...].astype(BF))
    pack[0] = grid[:, 0:192]
    for q, (host, at) in enumerate(IN_PLACES):
        pack[0, host * XB:(host + 1) * XB, at * JB:(at + 1) * JB] = grid[q * XB:(q + 1) * XB, 192:216]
    lane = iota((1, JB * SEC), 1)
    live = lo * JB + lane // SEC < sizes_by_sector(sizes, lane % SEC, 0)
    row = up * XB + iota((XB, 1), 0)
    limit = {c: sizes_by_sector(sizes, lane % SEC, c) for c in sorted(set(CHARGE))}
    blank = jnp.zeros((4, JB * SEC), F32)
    for k in range(DD):
        keep = live & (row < limit[CHARGE[k]])
        up_s[0, k * 16:k * 16 + XB, :] = jnp.where(keep, upper[k].astype(F32), 0.0)
        up_s[0, k * 16 + XB:(k + 1) * 16, :] = blank
        up_s[1, k * 16:k * 16 + XB, :] = jnp.where(keep, lower[k].astype(F32), 0.0)
        up_s[1, k * 16 + XB:(k + 1) * 16, :] = blank
    a, b = iota((128, 144), 0), iota((128, 144), 1)
    dense = nn(one_hot((b == (a // XB) * 16 + a % XB) & (a < 108)), up_s[0].astype(BF)).astype(BF)
    a, b = iota((192, 192), 0), iota((192, 192), 1)
    edge = nt(one_hot(b == (a % JB) * SEC + a // JB), dense).astype(BF)
    a, b = iota((DD * 96, 144), 0), iota((DD * 96, 144), 1)
    pos = a // 96
    l = jnp.where(pos == 4, ORDER[4], jnp.where(pos == 5, ORDER[5], pos))
    copies = nn(one_hot(b == l * 16 + a % XB), up_s[1].astype(BF))
    sector = iota((96, 192), 0) // XB - iota((96, 192), 1) % SEC
    for n, l in enumerate(ORDER):
        wide_s[n * 96:(n + 1) * 96, :] = jnp.where(
            sector == CHARGE[l], copies[n * 96:(n + 1) * 96], 0.0
        ).astype(BF)
    a, b = iota((192, 128), 0), iota((192, 128), 1)
    folded = nn(wide_s[...], one_hot(b == a // SEC))
    for n in range(SEC):
        pack[1, :, n * JB:(n + 1) * JB] = folded[n * 96:(n + 1) * 96, 0:JB]
    for v, (host, at) in enumerate(OUT_PLACES):
        row = SEC * 96 + v * XB
        pack[1, host * XB:(host + 1) * XB, at * JB:(at + 1) * JB] = folded[row:row + XB, 0:JB]
    near = pack[:, :, 0:128].astype(BF)
    far = pack[:, :, 128:192].astype(BF)
    rest = [jnp.concatenate([far[side, 0:48], far[side, 48:96]], axis=1) for side in range(2)]
    for n in range(NY):
        for side in range(2):
            lb_out[n, side, 0:96, :] = near[side]
            lb_out[n, side, 96:144, :] = rest[side]
    u_out[...] = edge


def prepare(sizes, left, upper, lower):
    return pl.pallas_call(
        prepare_kernel,
        out_shape=(
            jax.ShapeDtypeStruct((NY, 2, 144, 128), BF),
            jax.ShapeDtypeStruct((192, 128), BF),
        ),
        in_specs=[SMEM, VMEM, VMEM, VMEM],
        out_specs=(VMEM, VMEM),
        scratch_shapes=[
            pltpu.VMEM((216, 96), F32),
            pltpu.VMEM((2, 144, 192), F32),
            pltpu.VMEM((DD * 96, 192), BF),
            pltpu.VMEM((2, 96, 192), F32),
        ],
        compiler_params=WIDE,
        name="prepare",
    )(sizes, left, upper, lower)


def charge_of(member):
    return member // 3 - member % 3


def regrouping(turn, count):
    a, b = iota((count * 96, 384), 0), iota((count * 96, 384), 1)
    size = count * XB
    d = ((a % size) // XB + turn + NX - lax.axis_index("up") % NX) % NX
    return one_hot(b == d * 96 + (a // size) * XB + a % XB)


def regrouped(regroup, pieces, g):
    lines = [piece[g] for piece in pieces]
    near = jnp.concatenate([line[0:96, :] for line in lines], axis=0)
    far = jnp.concatenate(
        [line[96:144, 64 * h:64 * (h + 1)] for line in lines for h in range(2)], axis=0
    )
    return nn(regroup, jnp.concatenate([near, far], axis=1)).astype(BF)


def spread_out(part, charge, hosts, sector):
    lane = iota((1, 192), 1) // JB
    size = part.shape[0] // SEC
    rows = part[sector * size:(sector + 1) * size]
    for n in range(SEC):
        if not 0 <= sector + charge[ORDER[n]] < SEC:
            rows = jnp.where(lane == n, jnp.zeros((), BF), rows)
    host, spot = hosts[sector]
    return rows, part[host * size:(host + 1) * size, spot * JB:(spot + 1) * JB]


def mix_kernel(site, u, own, right, far, left, spread, left_q, image, moved, merged, mixed, legs):
    regroup = regrouping(0, NX)
    left_q[...] = jnp.zeros(left_q.shape, BF)
    moved[...] = jnp.zeros(moved.shape, F32)
    for g in range(NY):
        part = regrouped(regroup, (own, right, far, left), g)
        for q in range(SEC):
            rows, last = spread_out(part, CHARGE, IN_PLACES, q)
            left_q[q, g * 48:(g + 1) * 48, 0:192] = rows
            left_q[q, g * 48:(g + 1) * 48, 192:216] = last
    for q in range(SEC):
        columns = u[:, q * JB:(q + 1) * JB, :].reshape(CAP, 128)
        image[q * 128:(q + 1) * 128, :] = tn(columns, left_q[q]).astype(BF)
    a, b = iota((256, 384), 0), iota((256, 384), 1)
    inside = b % 128
    order = one_hot((a == (inside // 8) * JB + (b // 128) * 8 + inside % 8) & (inside < 72))
    parted = nn(image[...], order)
    for q in range(SEC):
        for k in range(DD):
            p = q + CHARGE[k]
            if 0 <= p < SEC:
                rows = parted[q * 128 + k * XB:q * 128 + (k + 1) * XB]
                for part in range(3):
                    moved[part * 128 + p * XB:part * 128 + (p + 1) * XB, k * 128:(k + 1) * 128] = (
                        rows[:, part * 128:(part + 1) * 128]
                    )
    legs[...] = jnp.zeros(legs.shape, F32)
    for n in range(DD * DD):
        legs[n * 16:n * 16 + DD, 0:DD] = site[n // DD, n % DD]
    a, b = iota((88, DD * 128), 0), iota((88, DD * 128), 1)
    pos = (b % 128) // 8
    s = jnp.where(pos == 4, ORDER[4], jnp.where(pos == 5, ORDER[5], pos))
    widen = one_hot((s + (b // 128) * DD == a) & (pos < DD))
    l, b = iota((16, DD * 128), 0), iota((16, DD * 128), 1)
    pos = (b % 128) // 8
    s = jnp.where(pos == 4, ORDER[4], jnp.where(pos == 5, ORDER[5], pos))
    balance = charge_of(b // 128) - charge_of(s) - charge_of(l)
    wide = []
    for r in range(DD):
        rows = tn(legs[pl.ds(r, 88, stride=16), :].astype(BF), widen)[0:16]
        wide.append(jnp.where(balance == -CHARGE[r], rows, 0.0))
    a, b = iota((8, DD * 128), 0), iota((8, DD * 128), 1)
    same = (b % 8 == a) & (b % 128 < 72)
    weights = [
        jnp.where(same, wide[r][l:l + 1, :], 0.0) for r in ORDER for l in ORDER
    ]
    weights = jnp.concatenate(weights, axis=0).astype(BF)
    product = nt(weights, moved[...].astype(BF))
    for n in range(DD):
        for part in range(3):
            block = product[n * 72:(n + 1) * 72, part * 128:part * 128 + 96].reshape(DD, 8, 96)
            if n < SEC:
                merged[:, part, :, n * 96:(n + 1) * 96] = block
                continue
            for p, (host, spot) in enumerate(IN_PLACES):
                start = spot * 96 + host * XB
                merged[:, part, :, start:start + XB] = block[:, :, p * XB:(p + 1) * XB]
    mixed[0:216, :] = merged[...].reshape(216, SEC * 96).astype(BF)
    mixed[216:256, :] = jnp.zeros((40, SEC * 96), BF)
    lane = iota((1, SEC * 96), 1)
    sector = (lane % 96) // XB
    for n in range(SEC):
        sector = jnp.where(lane // 96 == n, sector + CHARGE[ORDER[n]], sector)
    for p, (host, spot) in enumerate(IN_PLACES):
        sector = jnp.where(lane // XB == spot * SEC + host, p, sector)
    for v in range(SEC):
        spread[v * 256:(v + 1) * 256, :] = jnp.where(sector == v, mixed[...], jnp.zeros((), BF))


def mix(site, u, pieces):
    return pl.pallas_call(
        mix_kernel,
        out_shape=jax.ShapeDtypeStruct((SEC * 256, SEC * 96), BF),
        in_specs=[VMEM] * 6,
        out_specs=VMEM,
        scratch_shapes=[
            pltpu.VMEM((SEC, CAP, 256), BF),
            pltpu.VMEM((SEC * 128, 256), BF),
            pltpu.VMEM((3 * 128, DD * 128), F32),
            pltpu.VMEM((DD, 3, 8, SEC * 96), F32),
            pltpu.VMEM((256, SEC * 96), BF),
            pltpu.VMEM((89 * 16, 128), F32),
        ],
        compiler_params=PARAMS,
        cost_estimate=pl.CostEstimate(flops=6_000_000_000, bytes_accessed=3_000_000, transcendentals=0),
        name="mix",
    )(site, u, *pieces)


def lower_kernel(half, spread, own, right, far, left, out, lower_v):
    regroup = regrouping(2 * lax.rem(lax.axis_index("lo") + half, 2), 2)
    lower_v[...] = jnp.zeros(lower_v.shape, BF)
    for g in range(NY):
        part = regrouped(regroup, (own, right, far, left), g)
        for v in range(SEC):
            rows, last = spread_out(part, [-c for c in CHARGE], OUT_PLACES, v)
            lower_v[g * JB:(g + 1) * JB, v * 256:v * 256 + 192] = rows
            lower_v[g * JB:(g + 1) * JB, v * 256 + 192:v * 256 + 216] = last
    for n in range(3):
        cut = slice(n * 256, (n + 1) * 256)
        total = nn(lower_v[...], spread[:, cut])
        out[:, :, cut] = total.reshape(NY, JB, 256).astype(out.dtype)


def contract_lower(half, spread, pieces):
    return pl.pallas_call(
        functools.partial(lower_kernel, half),
        out_shape=jax.ShapeDtypeStruct((NY, JB, SEC * 96), BF if half else F32),
        in_specs=[VMEM] * 5,
        out_specs=VMEM,
        scratch_shapes=[pltpu.VMEM((NY * JB, SEC * 256), BF)],
        compiler_params=PARAMS,
        cost_estimate=pl.CostEstimate(flops=3_000_000_000, bytes_accessed=3_000_000, transcendentals=0),
        name="lower_theirs" if half else "lower_ours",
    )(spread, *pieces)


def finish_kernel(terms, out, stacked):
    total = terms[0].astype(F32)
    for z in range(1, N_LO // 2):
        total = total + terms[z].astype(F32)
    for n in range(SEC):
        r = ORDER[n]
        stacked[r * JB:(r + 1) * JB, :] = total[:, n * 96:(n + 1) * 96]
    for p, (host, spot) in enumerate(IN_PLACES):
        start = spot * 96 + host * XB
        stacked[SEC * JB:DD * JB, p * XB:(p + 1) * XB] = total[:, start:start + XB]
    a, b = iota((96, 96), 0), iota((96, 96), 1)
    turned = nn(stacked[...].astype(BF), one_hot(b == (a % XB) * SEC + a // XB))
    p = iota((1, 96), 1) % SEC
    for r in range(DD):
        keep = (p + CHARGE[r] >= 0) & (p + CHARGE[r] < SEC)
        out[r] = jnp.where(keep, turned[r * JB:(r + 1) * JB, :], 0.0).astype(BF)


def finish(terms):
    return pl.pallas_call(
        finish_kernel,
        out_shape=jax.ShapeDtypeStruct((DD, JB, 96), BF),
        in_specs=[VMEM],
        out_specs=VMEM,
        scratch_shapes=[pltpu.VMEM((DD * JB, 96), F32)],
        compiler_params=PARAMS,
        name="finish",
    )(terms)


Z_GROUPS = [[2 * z + core for z in range(N_LO // 2)] for core in range(2)]
Y_GROUPS = [[y * NX + x for y in range(NY)] for x in range(NX)]


def from_x(value, d):
    pairs = [(y * NX + x, y * NX + (x - d) % NX) for y in range(NY) for x in range(NX)]
    return lax.ppermute(value, "up", pairs)


def local(sector_sizes, left, upper_edge, lower_edge, site_block):
    lb, u = prepare(sector_sizes, left, upper_edge, lower_edge)
    line = lax.all_to_all(lb, "up", 0, 0, axis_index_groups=Y_GROUPS)
    u = lax.all_gather(u, "lo", axis=0)
    line, u = lax.optimization_barrier((line, u))
    left, lower = line[:, 0], line[:, 1]
    left_right, left_left = from_x(left, 1), from_x(left, -1)
    lower_right, lower_left = from_x(lower, 1), from_x(lower, -1)
    left_far, lower_far = from_x(left_right, 1), from_x(lower_left, -1)
    spread = mix(site_block, u, (left, left_right, left_far, left_left))
    lines = (lower, lower_right, lower_far, lower_left)
    theirs = contract_lower(1, spread, lines)
    ours = contract_lower(0, spread, lines)
    swap = [(n, n + 1 - 2 * (n % 2)) for n in range(N_LO)]
    theirs = lax.ppermute(theirs, "lo", swap)
    terms = (ours + theirs.astype(F32)).astype(BF)
    terms = lax.all_to_all(terms, "lo", 0, 0, axis_index_groups=Z_GROUPS)
    return finish(terms)


def solution(mesh):
    return jax.shard_map(
        local,
        mesh=mesh,
        in_specs=(P(), P(None, "lo", "up"), P(None, "up", "lo"), P(None, "up", "lo"), P()),
        out_specs=P(None, "lo", "up"),
        check_vma=False,
    )
```
